512 devices in a mesh: cuts: 32 (over x, y), col: 16 (over z, core).
Axes of the slice: x: 4, y: 8, z: 8, core: 2. Of those that a mesh axis runs over, the one named last changes fastest.
Arguments:
- levels: int32 [64, 1024], P('cuts'), may hold values from 0 to 65535
- start_basis: float32 [32, 1024, 2048], P('cuts', 'col'), may hold values from -6 to 6
Outputs:
- exponents: float32 [1024], P('col')
- running_means: float32 [1024], P('col')
- handed: float32 [32, 1024, 2048], P('cuts', 'col')
The draws below stay inside these ranges and needn't reach their ends.
All inputs are finite; a program needn't handle non-finite values.
Results may differ from the reference program's by a relative error of at most 0.0009.
Values sent between devices are 32-bit elements; how exact they have to be, the bound alone decides.
A program may use at most 64 MiB of HBM per device.

```python
import math
import jax
import jax.numpy as jnp
from jax import lax

M = 32
K = 1024
SLICES = 2
SITES = 1024
ROWS = 2048
TOTAL_SLICES = 64
N_CUTS = 32


def with_ends(drawn, stream_key, smallest, high):
    spot = [jax.random.randint(jax.random.fold_in(stream_key, axis), (), 0, length) for axis, length in enumerate(drawn.shape)]
    longest = drawn.shape.index(max(drawn.shape))
    neighbour = spot[:longest] + [(spot[longest] + 1) % drawn.shape[longest]] + spot[longest + 1:]
    return drawn.at[tuple(spot)].set(smallest).at[tuple(neighbour)].set(high)


def block_levels(key, shape, pieces, low, largest):
    factor_of, own = 1.0, jax.random.fold_in(key, 6)
    for position, parts in pieces:
        draws = jnp.exp(jax.random.uniform(jax.random.fold_in(own, position), (parts,), jnp.float32, low / len(pieces), largest / len(pieces)))
        factor_of = factor_of * jnp.repeat(draws, shape[position] // parts).reshape([-1 if axis == position else 1 for axis in range(len(shape))])
    return factor_of


def centred(rng, shape, scale, bound, cuts=(), kind=jnp.bfloat16):
    drawn = scale * jax.random.normal(rng, shape, jnp.float32)
    if cuts:
        drawn = drawn * block_levels(rng, shape, cuts, -0.22, 0.18)
    return jnp.clip(drawn, -bound, bound).astype(kind)


def setup_inputs(seed: int = 0) -> dict:
    arg_keys = jax.random.split(jax.random.key(seed), 3)
    levels = with_ends(jax.random.randint(arg_keys[0], (TOTAL_SLICES, SITES), 0, 65536), jax.random.fold_in(arg_keys[0], 1), 0, 65535).astype(jnp.int32)
    start_basis = centred(arg_keys[1], (N_CUTS, K, ROWS), 1.0, 6.0, ((0, 32), (1, 16)), jnp.float32)
    return {"levels": levels, "start_basis": start_basis}


energy = 0.5
disorder = 4.0
level_span = 65536.0

def neighbours(signal):
    grid = signal.reshape(signal.shape[:-1] + (M, M))
    summed = jnp.roll(grid, 1, -1) + jnp.roll(grid, -1, -1) + jnp.roll(grid, 1, -2) + jnp.roll(grid, -1, -2)
    return summed.reshape(signal.shape)

def segment(inputs):
    seg_levels, seg_start = inputs
    upper = seg_start[:, :SITES]
    lower = seg_start[:, SITES:]
    for sweep_index in range(SLICES):
        onsite = disorder * (seg_levels[sweep_index].astype(seg_start.dtype) / level_span - 0.5)
        advanced = (energy - onsite) * upper - neighbours(upper) - lower
        lower = upper
        upper = advanced
    propagated = jnp.concatenate([upper, lower], axis=1)
    gram_matrix = jnp.dot(propagated, propagated.T, precision=lax.Precision.HIGHEST)
    factor = jnp.linalg.cholesky(gram_matrix)
    log_pivots = jnp.log(jnp.diagonal(factor)) - 0.5 * math.log(ROWS)
    basis_out = jax.scipy.linalg.solve_triangular(factor, propagated, lower=True) * math.sqrt(ROWS)
    return (log_pivots, basis_out)

def reference(levels, start_basis):
    grouped = levels.reshape(N_CUTS, SLICES, SITES)
    log_pivots, basis_out = lax.map(segment, (grouped, start_basis))
    exponents = lax.optimization_barrier(jnp.sum(log_pivots, axis=0)) / (SLICES * N_CUTS)
    counts_up = jnp.arange(1, K + 1).astype(exponents.dtype)
    running_means = jnp.cumsum(exponents) / counts_up
    handed = jnp.concatenate([start_basis[:1], basis_out[:-1]], axis=0)
    return (exponents, running_means, handed)
```

```python
import functools
import math

import jax
import jax.numpy as jnp
from jax import lax
from jax.experimental import pallas as pl
from jax.experimental.pallas import tpu as pltpu
from jax.sharding import PartitionSpec as P

M = 32
SITES = 1024
ROWS = 2048
SLICES = 2
B = 128
HALF = 64
CHIPS = 8
COL = 16
K = 1024
BANDS = 5 * B

energy = 0.5
disorder = 4.0
level_span = 65536.0

MESH = pl.DeviceIdType.MESH
VMEM = pl.BlockSpec(memory_space=pltpu.VMEM)
f32 = jnp.float32


def dot(a, b, ca, cb):
    return lax.dot_general(
        a, b, (((ca,), (cb,)), ((), ())), precision=lax.Precision.HIGHEST, preferred_element_type=f32
    )


def remote(src, dst, send, recv, device):
    return pltpu.make_async_remote_copy(
        src_ref=src, dst_ref=dst, send_sem=send, recv_sem=recv, device_id=device, device_id_type=MESH
    )


def neighbours(x):
    site = lax.broadcasted_iota(jnp.int32, x.shape, 1)
    b = lax.rem(site, M)
    around = lambda by: pltpu.roll(x, by % SITES, 1)
    along = jnp.where(b == 0, around(1 - M), around(1)) + jnp.where(b == M - 1, around(M - 1), around(-1))
    return along + around(M) + around(-M)


def gram_kernel(
    lev, start, slab, gall, prop, gat, part, other,
    gs, gr, fs, als, alr, ps, pr, ags, agr, ins, inr,
):
    me = lax.axis_index("col")
    z, h = me // 2, me % 2
    up, down = lax.rem(z + 1, CHIPS), lax.rem(z + CHIPS - 1, CHIPS)
    partner = z * 2 + 1 - h
    mine = pl.ds(pl.multiple_of(h * HALF, HALF), HALF)
    theirs = pl.ds(pl.multiple_of((1 - h) * HALF, HALF), HALF)

    barrier = pltpu.get_barrier_semaphore()
    for o in range(1, COL):
        pl.semaphore_signal(barrier, inc=1, device_id={"col": lax.rem(me + o, COL)}, device_id_type=MESH)

    upper = start[:, :SITES]
    lower = start[:, SITES:]
    for n in range(SLICES):
        onsite = disorder * (lev[n : n + 1, :].astype(f32) / level_span - 0.5)
        upper, lower = (energy - onsite) * upper - neighbours(upper) - lower, upper
    prop[:, :SITES] = upper
    prop[:, SITES:] = lower
    pl.semaphore_wait(barrier, COL - 1)

    halves = [prop.at[:, pl.ds(g * SITES, SITES)] for g in range(2)]
    sends = []
    for g in range(2):
        sends.append(remote(halves[g], gat.at[1, mine], gs.at[g], gr.at[2 + h], {"col": up * 2 + g}))
        sends.append(remote(halves[g], gat.at[3, mine], gs.at[2 + g], gr.at[6 + h], {"col": down * 2 + g}))
    for s in sends:
        s.start()
    own_half = pl.ds(pl.multiple_of(h * SITES, SITES), SITES)
    their_half = pl.ds(pl.multiple_of((1 - h) * SITES, SITES), SITES)
    swap = remote(prop.at[:, their_half], gat.at[0, mine], gs.at[4], gr.at[h], {"col": partner})
    swap.start()
    sends.append(swap)
    gat[0, mine, :] = prop[:, own_half]

    def arrived(slot, s):
        rows = pl.ds(s * HALF, HALF)
        remote(gat.at[slot, rows], gat.at[slot, rows], gs.at[0], gr.at[2 * slot + s], {"col": partner}).wait_recv()

    for s in range(2):
        rows = pl.ds(s * HALF, HALF)
        arrived(1, s)
        f = remote(gat.at[1, rows], gat.at[2, rows], fs.at[s], gr.at[4 + s], {"col": up * 2 + h})
        f.start()
        sends.append(f)
        arrived(3, s)
        f = remote(gat.at[3, rows], gat.at[4, rows], fs.at[2 + s], gr.at[8 + s], {"col": down * 2 + h})
        f.start()
        sends.append(f)

    my_rows = pl.ds(pl.multiple_of(me * HALF, HALF), HALF)
    for o in range(1, COL):
        d = lax.rem(me + o, COL)
        s = remote(
            prop.at[:, pl.ds(pl.multiple_of(d * B, B), B)], slab.at[my_rows], als.at[o], alr.at[o], {"col": d}
        )
        s.start()
        sends.append(s)
    slab[my_rows, :] = prop[:, pl.ds(pl.multiple_of(me * B, B), B)]

    remote(gat.at[0, theirs], gat.at[0, theirs], gs.at[0], gr.at[1 - h], {"col": partner}).wait_recv()
    part[:, 0:B] = dot(gat[0], gat[0], 1, 1)
    part[:, B : 2 * B] = dot(gat[0], gat[3], 1, 1)
    for s in range(2):
        arrived(2, s)
        arrived(4, s)
    part[:, 2 * B : 3 * B] = dot(gat[0], gat[4], 1, 1)
    part[:, 3 * B : 4 * B] = dot(gat[1], gat[4], 1, 1)
    part[:, 4 * B : 5 * B] = dot(gat[2], gat[4], 1, 1)

    both = remote(part.at[theirs], other, ps, pr, {"col": partner})
    both.start()
    both.wait_recv()
    sends.append(both)
    gall[z, mine, :] = part[mine, :] + other[...]

    def inside(chip, rows, i):
        s = remote(gall.at[chip, rows], gall.at[chip, rows], ins.at[i], inr.at[i], {"col": partner})
        s.start()
        sends.append(s)

    quarter = HALF // 2
    first = pl.ds(pl.multiple_of(h * HALF, quarter), quarter)
    second = pl.ds(pl.multiple_of(h * HALF + quarter, quarter), quarter)
    for d in range(1, 5):
        behind, ahead = lax.rem(z + CHIPS - d, CHIPS), lax.rem(z + d, CHIPS)
        cw_chip, cc_chip = lax.rem(z + CHIPS - d + 1, CHIPS), lax.rem(z + d - 1, CHIPS)
        cw_rows, cc_rows = (mine, mine) if d < 4 else (first, second)
        cw = remote(
            gall.at[cw_chip, cw_rows], gall.at[cw_chip, cw_rows], ags.at[d], agr.at[d], {"col": up * 2 + h}
        )
        cc = remote(
            gall.at[cc_chip, cc_rows], gall.at[cc_chip, cc_rows], ags.at[4 + d], agr.at[4 + d], {"col": down * 2 + h}
        )
        cw.start()
        cc.start()
        if d == 1:
            inside(z, mine, 0)
        sends += [cw, cc]
        remote(gall.at[behind, cw_rows], gall.at[behind, cw_rows], gs.at[0], agr.at[d], {"col": partner}).wait_recv()
        inside(behind, cw_rows, d)
        remote(gall.at[ahead, cc_rows], gall.at[ahead, cc_rows], gs.at[0], agr.at[4 + d], {"col": partner}).wait_recv()
        inside(ahead, cc_rows, 4 + d)

    t_first = pl.ds(pl.multiple_of((1 - h) * HALF, quarter), quarter)
    t_second = pl.ds(pl.multiple_of((1 - h) * HALF + quarter, quarter), quarter)
    for d in range(0, 5):
        behind, ahead = lax.rem(z + CHIPS - d, CHIPS), lax.rem(z + d, CHIPS)
        cw_rows, cc_rows = (theirs, theirs) if d < 4 else (t_first, t_second)
        remote(gall.at[behind, cw_rows], gall.at[behind, cw_rows], gs.at[0], inr.at[d], {"col": partner}).wait_recv()
        if d:
            remote(gall.at[ahead, cc_rows], gall.at[ahead, cc_rows], gs.at[0], inr.at[4 + d], {"col": partner}).wait_recv()
    for o in range(1, COL):
        rows = pl.ds(pl.multiple_of(lax.rem(me + COL - o, COL) * HALF, HALF), HALF)
        remote(slab.at[rows], slab.at[rows], gs.at[0], alr.at[o], {"col": partner}).wait_recv()
    for s in sends:
        s.wait_send()


def eliminate(d, out):
    tiles = [d[8 * t : 8 * t + 8, :] for t in range(B // 8)]
    last = len(tiles) - 1
    lane = lax.broadcasted_iota(jnp.int32, (8, B), 1)
    row = lambda v, i: jnp.broadcast_to(v[i : i + 1, :], (8, B))
    col = lambda v, c: jnp.broadcast_to(v[:, c : c + 1], (8, B))
    for q, tile in enumerate(tiles):
        tile = tiles[q]
        c0 = 8 * q
        rows = [row(tile, j) for j in range(8)]
        a = {(m, j): col(rows[m], c0 + j) for m in range(8) for j in range(m, 8)}
        block = jnp.logical_and(lane >= c0, lane < c0 + 8)
        e = [jnp.where(block, jnp.where(lane == c0 + j, 1.0, 0.0), rows[j]) for j in range(8)]
        f0, f1, w = {}, {}, [None] * 8
        for i in range(0, 8, 2):
            k = i + 1
            p, r, s = a[i, i], a[i, k], a[k, k]
            over = 1.0 / (p * s - r * r)
            for j in range(k + 1, 8):
                x, y = a[i, j], a[k, j]
                f0[i, j] = (s * x - r * y) * over
                f1[i, j] = (p * y - r * x) * over
                for m in range(j, 8):
                    a[j, m] = a[j, m] - (f0[i, j] * a[i, m] + f1[i, j] * a[k, m])
                e[j] = e[j] - (f0[i, j] * e[i] + f1[i, j] * e[k])
            w[i] = (s * e[i] - r * e[k]) * over
            w[k] = (p * e[k] - r * e[i]) * over
        if q < last:
            for i in (4, 2, 0):
                for j in range(i + 2, 8):
                    w[i] = w[i] - f0[i, j] * w[j]
                    w[i + 1] = w[i + 1] - f1[i, j] * w[j]
            for t in range(q + 1, last + 1):
                s = [col(tiles[t], c0 + j) * w[j] for j in range(8)]
                s = ((s[0] + s[1]) + (s[2] + s[3])) + ((s[4] + s[5]) + (s[6] + s[7]))
                tiles[t] = jnp.where(block, 0.0, tiles[t]) - s
        for i in range(0, 8, 2):
            k = i + 1
            p, r, s = a[i, i], a[i, k], a[k, k]
            ratio = r / p
            first = e[i] * lax.rsqrt(p)
            second = (e[k] - ratio * e[i]) * lax.rsqrt(s - ratio * r)
            out[c0 + i : c0 + i + 1, :] = jnp.where(lane <= c0 + i, first, 0.0)[0:1]
            out[c0 + k : c0 + k + 1, :] = jnp.where(lane <= c0 + k, second, 0.0)[0:1]


def factor_kernel(gall, slab, x, piv, w, inv, r):
    blocks = K // B
    at = lambda i: slice(i * B, i * B + B)
    band = lambda chip, d: gall[chip % CHIPS, :, at(d)]
    for i in range(blocks):
        for j in range(i, blocks):
            d = j - i
            if d <= 2:
                g = band(i, d)
            elif d == 3:
                g = band(i + 1, 3)
            elif d == 4:
                g = band(i + 2, 4)
            elif d == 5:
                g = band(j + 1, 3).T
            else:
                g = band(j, 8 - d).T
            w[at(i), at(j)] = g
    w[:, K:] = slab[...]
    eye = lax.broadcasted_iota(jnp.int32, (B, B), 0) == lax.broadcasted_iota(jnp.int32, (B, B), 1)
    scale = math.sqrt(ROWS)

    @pl.loop(0, blocks)
    def _(k):
        r0 = pl.multiple_of(k * B, B)
        eliminate(w[pl.ds(r0, B), pl.ds(r0, B)], inv)
        li = inv[...]
        diagonal = jnp.sum(jnp.where(eye, li, 0.0), axis=0, keepdims=True)
        piv[pl.ds(k, 1), :] = -jnp.log(diagonal) - 0.5 * math.log(ROWS)
        for kk in range(blocks):

            @pl.when(k == kk)
            def _():
                lo = kk * B
                r[:, lo + B :] = dot(li, w[lo : lo + B, lo + B :], 1, 0)
                for i in range(kk + 1, blocks):
                    w[at(i), i * B :] -= dot(r[:, at(i)], r[:, i * B :], 0, 0)
                x[at(kk), :] = r[:, K:] * scale


def hand_kernel(cuts, x, start, piv, handed, exponents, running, allp, xs, xr, vs, vr):
    me = lax.axis_index("col")
    c = lax.axis_index("cuts")
    barrier = pltpu.get_barrier_semaphore()
    for o in range(1, cuts):
        pl.semaphore_signal(
            barrier, inc=1, device_id={"cuts": lax.rem(c + o, cuts), "col": me}, device_id_type=MESH
        )

    @pl.when(c > 0)
    def _():
        for i in range(COL):
            pl.semaphore_signal(barrier, inc=1, device_id={"cuts": c - 1, "col": i}, device_id_type=MESH)

    pl.semaphore_wait(barrier, jnp.where(c < cuts - 1, cuts - 1 + COL, cuts - 1))

    my_cols = pl.ds(pl.multiple_of(me * B, B), B)
    give = []
    for o in range(1, cuts):
        s = remote(piv, allp.at[c], vs.at[o], vr.at[o], {"cuts": lax.rem(c + o, cuts), "col": me})
        s.start()
        give.append(s)
    allp[c] = piv[...]

    @pl.when(c < cuts - 1)
    def _():
        for o in range(COL):
            i = lax.rem(me + o, COL)
            remote(
                x.at[pl.ds(pl.multiple_of(i * HALF, HALF), HALF)], handed.at[:, my_cols],
                xs.at[o], xr.at[o], {"cuts": c + 1, "col": i},
            ).start()

    @pl.when(c == 0)
    def _():
        handed[...] = start[...]

    for o in range(1, cuts):
        come = allp.at[lax.rem(c + cuts - o, cuts)]
        remote(come, come, vs.at[o], vr.at[o], {"cuts": lax.rem(c + o, cuts), "col": me}).wait_recv()
    total = allp[0]
    for o in range(1, cuts):
        total = total + allp[o]
    expo = total / (SLICES * cuts)
    lane = lax.broadcasted_iota(jnp.int32, (B, B), 1)
    upto = jnp.where(lax.broadcasted_iota(jnp.int32, (B, B), 0) <= lane, 1.0, 0.0).astype(f32)
    sums = dot(expo, upto, 1, 0)
    before = jnp.zeros((1, 1), f32)
    parts = []
    for i in range(K // B):
        parts.append(sums[i : i + 1, :] + before)
        before = before + sums[i : i + 1, B - 1 : B]
    cumulated = jnp.concatenate(parts, axis=0)
    place = lax.broadcasted_iota(jnp.int32, (K // B, B), 0) * B + lax.broadcasted_iota(jnp.int32, (K // B, B), 1)
    means = cumulated / (place + 1).astype(f32)
    here = lax.broadcasted_iota(jnp.int32, (K // B, B), 0) == me // 2
    for value, out in ((expo, exponents), (means, running)):
        line = jnp.sum(jnp.where(here, value, 0.0), axis=0, keepdims=True)
        out[...] = jnp.where(me % 2 == 0, line[:, :HALF], line[:, HALF:])

    @pl.when(c > 0)
    def _():
        for o in range(COL):
            j = lax.rem(me + COL - o, COL)
            come = handed.at[:, pl.ds(pl.multiple_of(j * B, B), B)]
            remote(come, come, xs.at[o], xr.at[o], {"cuts": c - 1, "col": j}).wait_recv()

    @pl.when(c < cuts - 1)
    def _():
        for o in range(COL):
            i = lax.rem(me + o, COL)
            rows = x.at[pl.ds(pl.multiple_of(i * HALF, HALF), HALF)]
            remote(rows, handed.at[:, my_cols], xs.at[o], xr.at[o], {"cuts": c + 1, "col": i}).wait_send()

    for s in give:
        s.wait_send()


def local(cuts, levels, start_basis):
    start = start_basis[0]
    dma = pltpu.SemaphoreType.DMA
    slab, gall = pl.pallas_call(
        gram_kernel,
        out_shape=(jax.ShapeDtypeStruct((K, B), f32), jax.ShapeDtypeStruct((CHIPS, B, BANDS), f32)),
        in_specs=[VMEM] * 2,
        out_specs=(VMEM,) * 2,
        scratch_shapes=[
            pltpu.VMEM((HALF, ROWS), f32),
            pltpu.VMEM((5, B, SITES), f32),
            pltpu.VMEM((B, BANDS), f32),
            pltpu.VMEM((HALF, BANDS), f32),
            dma((5,)), dma((10,)), dma((4,)), dma((COL,)), dma((COL,)),
            dma, dma, dma((9,)), dma((9,)), dma((9,)), dma((9,)),
        ],
        compiler_params=pltpu.CompilerParams(
            collective_id=1, has_side_effects=True, vmem_limit_bytes=32 << 20
        ),
        name="gram",
    )(levels, start)
    x, piv = pl.pallas_call(
        factor_kernel,
        out_shape=(jax.ShapeDtypeStruct((K, B), f32), jax.ShapeDtypeStruct((K // B, B), f32)),
        in_specs=[VMEM] * 2,
        out_specs=(VMEM,) * 2,
        scratch_shapes=[pltpu.VMEM((K, K + B), f32), pltpu.VMEM((B, B), f32), pltpu.VMEM((B, K + B), f32)],
        compiler_params=pltpu.CompilerParams(vmem_limit_bytes=32 << 20),
        name="factor",
    )(gall, slab)
    handed, exponents, running = pl.pallas_call(
        functools.partial(hand_kernel, cuts),
        out_shape=(
            jax.ShapeDtypeStruct((HALF, ROWS), f32),
            jax.ShapeDtypeStruct((1, HALF), f32),
            jax.ShapeDtypeStruct((1, HALF), f32),
        ),
        in_specs=[VMEM] * 3,
        out_specs=(VMEM,) * 3,
        scratch_shapes=[
            pltpu.VMEM((cuts, K // B, B), f32),
            dma((COL,)), dma((COL,)), dma((cuts,)), dma((cuts,)),
        ],
        compiler_params=pltpu.CompilerParams(
            collective_id=2, has_side_effects=True, vmem_limit_bytes=32 << 20
        ),
        name="hand",
    )(x, start, piv)
    return exponents[0], running[0], handed[None]


def solution(mesh):
    in_specs = (P("cuts", None), P("cuts", "col", None))
    out_specs = (P("col"), P("col"), P("cuts", "col", None))
    return jax.shard_map(
        functools.partial(local, mesh.shape["cuts"]), mesh=mesh, in_specs=in_specs, out_specs=out_specs, check_vma=False
    )
```

```python
import functools
import math

import jax
import jax.numpy as jnp
from jax import lax
from jax.experimental import pallas as pl
from jax.experimental.pallas import tpu as pltpu
from jax.sharding import PartitionSpec as P

M = 32
SITES = 1024
ROWS = 2048
SLICES = 2
B = 128
HALF = 64
CHIPS = 8
COL = 16
K = 1024
BANDS = 5 * B

energy = 0.5
disorder = 4.0
level_span = 65536.0

MESH = pl.DeviceIdType.MESH
VMEM = pl.BlockSpec(memory_space=pltpu.VMEM)
f32 = jnp.float32
bf16 = jnp.bfloat16


def dot(a, b, ca, cb):
    return lax.dot_general(
        a, b, (((ca,), (cb,)), ((), ())), precision=lax.Precision.HIGHEST, preferred_element_type=f32
    )


def remote(src, dst, send, recv, device):
    return pltpu.make_async_remote_copy(
        src_ref=src, dst_ref=dst, send_sem=send, recv_sem=recv, device_id=device, device_id_type=MESH
    )


def neighbours(x):
    site = lax.broadcasted_iota(jnp.int32, x.shape, 1)
    b = lax.rem(site, M)
    around = lambda by: pltpu.roll(x, by % SITES, 1)
    along = jnp.where(b == 0, around(1 - M), around(1)) + jnp.where(b == M - 1, around(M - 1), around(-1))
    return along + around(M) + around(-M)


def gram_kernel(
    lev, start, slab, gall, prop, gat, part, other,
    gs, gr, fs, als, alr, ps, pr, ags, agr, ins, inr,
):
    me = lax.axis_index("col")
    z, h = me // 2, me % 2
    up, down = lax.rem(z + 1, CHIPS), lax.rem(z + CHIPS - 1, CHIPS)
    partner = z * 2 + 1 - h
    mine = pl.ds(pl.multiple_of(h * HALF, HALF), HALF)
    theirs = pl.ds(pl.multiple_of((1 - h) * HALF, HALF), HALF)

    barrier = pltpu.get_barrier_semaphore()
    for o in range(1, COL):
        pl.semaphore_signal(barrier, inc=1, device_id={"col": lax.rem(me + o, COL)}, device_id_type=MESH)

    upper = start[:, :SITES]
    lower = start[:, SITES:]
    for n in range(SLICES):
        onsite = disorder * (lev[n : n + 1, :].astype(f32) / level_span - 0.5)
        upper, lower = (energy - onsite) * upper - neighbours(upper) - lower, upper
    prop[:, :SITES] = upper
    prop[:, SITES:] = lower
    pl.semaphore_wait(barrier, COL - 1)

    halves = [prop.at[:, pl.ds(g * SITES, SITES)] for g in range(2)]
    sends = []
    for g in range(2):
        sends.append(remote(halves[g], gat.at[1, mine], gs.at[g], gr.at[2 + h], {"col": up * 2 + g}))
        sends.append(remote(halves[g], gat.at[3, mine], gs.at[2 + g], gr.at[6 + h], {"col": down * 2 + g}))
    for s in sends:
        s.start()
    own_half = pl.ds(pl.multiple_of(h * SITES, SITES), SITES)
    their_half = pl.ds(pl.multiple_of((1 - h) * SITES, SITES), SITES)
    swap = remote(prop.at[:, their_half], gat.at[0, mine], gs.at[4], gr.at[h], {"col": partner})
    swap.start()
    sends.append(swap)
    gat[0, mine, :] = prop[:, own_half]

    def arrived(slot, s):
        rows = pl.ds(s * HALF, HALF)
        remote(gat.at[slot, rows], gat.at[slot, rows], gs.at[0], gr.at[2 * slot + s], {"col": partner}).wait_recv()

    for s in range(2):
        rows = pl.ds(s * HALF, HALF)
        arrived(1, s)
        f = remote(gat.at[1, rows], gat.at[2, rows], fs.at[s], gr.at[4 + s], {"col": up * 2 + h})
        f.start()
        sends.append(f)
        arrived(3, s)
        f = remote(gat.at[3, rows], gat.at[4, rows], fs.at[2 + s], gr.at[8 + s], {"col": down * 2 + h})
        f.start()
        sends.append(f)

    my_rows = pl.ds(pl.multiple_of(me * HALF, HALF), HALF)
    for o in range(1, COL):
        d = lax.rem(me + o, COL)
        s = remote(
            prop.at[:, pl.ds(pl.multiple_of(d * B, B), B)], slab.at[my_rows], als.at[o], alr.at[o], {"col": d}
        )
        s.start()
        sends.append(s)
    slab[my_rows, :] = prop[:, pl.ds(pl.multiple_of(me * B, B), B)]

    remote(gat.at[0, theirs], gat.at[0, theirs], gs.at[0], gr.at[1 - h], {"col": partner}).wait_recv()
    def lower(d, first, second):
        a = z if d < 3 else lax.rem(z + CHIPS + 2 - d, CHIPS)
        wraps = a + d >= CHIPS
        left = gat[jnp.where(wraps, first, second)]
        part[:, d * B : d * B + B] = dot(left, gat[jnp.where(wraps, second, first)], 1, 1)

    part[:, 0:B] = dot(gat[0], gat[0], 1, 1)
    lower(1, 0, 3)
    for s in range(2):
        arrived(2, s)
        arrived(4, s)
    lower(2, 0, 4)
    lower(3, 1, 4)
    lower(4, 2, 4)

    both = remote(part.at[theirs], other, ps, pr, {"col": partner})
    both.start()
    both.wait_recv()
    sends.append(both)
    gall[z, mine, :] = part[mine, :] + other[...]

    def inside(chip, rows, i):
        s = remote(gall.at[chip, rows], gall.at[chip, rows], ins.at[i], inr.at[i], {"col": partner})
        s.start()
        sends.append(s)

    quarter = HALF // 2
    first = pl.ds(pl.multiple_of(h * HALF, quarter), quarter)
    second = pl.ds(pl.multiple_of(h * HALF + quarter, quarter), quarter)
    for d in range(1, 5):
        behind, ahead = lax.rem(z + CHIPS - d, CHIPS), lax.rem(z + d, CHIPS)
        cw_chip, cc_chip = lax.rem(z + CHIPS - d + 1, CHIPS), lax.rem(z + d - 1, CHIPS)
        cw_rows, cc_rows = (mine, mine) if d < 4 else (first, second)
        cw = remote(
            gall.at[cw_chip, cw_rows], gall.at[cw_chip, cw_rows], ags.at[d], agr.at[d], {"col": up * 2 + h}
        )
        cc = remote(
            gall.at[cc_chip, cc_rows], gall.at[cc_chip, cc_rows], ags.at[4 + d], agr.at[4 + d], {"col": down * 2 + h}
        )
        cw.start()
        cc.start()
        if d == 1:
            inside(z, mine, 0)
        sends += [cw, cc]
        remote(gall.at[behind, cw_rows], gall.at[behind, cw_rows], gs.at[0], agr.at[d], {"col": partner}).wait_recv()
        inside(behind, cw_rows, d)
        remote(gall.at[ahead, cc_rows], gall.at[ahead, cc_rows], gs.at[0], agr.at[4 + d], {"col": partner}).wait_recv()
        inside(ahead, cc_rows, 4 + d)

    t_first = pl.ds(pl.multiple_of((1 - h) * HALF, quarter), quarter)
    t_second = pl.ds(pl.multiple_of((1 - h) * HALF + quarter, quarter), quarter)
    for d in range(0, 5):
        behind, ahead = lax.rem(z + CHIPS - d, CHIPS), lax.rem(z + d, CHIPS)
        cw_rows, cc_rows = (theirs, theirs) if d < 4 else (t_first, t_second)
        remote(gall.at[behind, cw_rows], gall.at[behind, cw_rows], gs.at[0], inr.at[d], {"col": partner}).wait_recv()
        if d:
            remote(gall.at[ahead, cc_rows], gall.at[ahead, cc_rows], gs.at[0], inr.at[4 + d], {"col": partner}).wait_recv()
    for o in range(1, COL):
        rows = pl.ds(pl.multiple_of(lax.rem(me + COL - o, COL) * HALF, HALF), HALF)
        remote(slab.at[rows], slab.at[rows], gs.at[0], alr.at[o], {"col": partner}).wait_recv()
    for s in sends:
        s.wait_send()


def tree(terms):
    while len(terms) > 1:
        pairs = [terms[i] + terms[i + 1] for i in range(0, len(terms) - 1, 2)]
        terms = pairs + terms[len(pairs) * 2 :]
    return terms[0]


def eliminate(d, out, one):
    tiles = [d[8 * t : 8 * t + 8, :] for t in range(B // 8)]
    last = len(tiles) - 1
    lane = lax.broadcasted_iota(jnp.int32, (8, B), 1)
    sub = lax.broadcasted_iota(jnp.int32, (8, B), 0)
    row = lambda v, i: jnp.broadcast_to(v[i : i + 1, :], (8, B))
    col = lambda v, c: jnp.broadcast_to(v[:, c : c + 1], (8, B))
    at = [sub == i for i in range(8)]
    pair = [jnp.logical_or(at[i], at[i + 1]) for i in range(0, 8, 2)]
    odd = sub % 2 == 1
    for q in range(last + 1):
        c0 = 8 * q
        block = jnp.logical_and(lane >= c0, lane < c0 + 8)
        v = [col(tiles[q], c0 + j) * one for j in range(8)]
        strip = jnp.where(block, jnp.where(lane - c0 == sub, 1.0, 0.0), tiles[q])
        rows = [row(strip, j) for j in range(8)]
        u = [None] * 8
        for p in range(4):
            i, k = 2 * p, 2 * p + 1
            a, r, e = row(v[i], i), row(v[i], k), row(v[k], k)
            over = 1.0 / (a * e - r * r)
            for j in range(i):
                u[j] = v[j] if u[j] is None else jnp.where(pair[p], v[j], u[j])
            if p == 0:
                pa, pr, pe = a, r, e
            else:
                pa, pr, pe = (jnp.where(pair[p], x, y) for x, y in ((a, pa), (r, pr), (e, pe)))
            if q == last and p == 3:
                break
            n0 = jnp.where(at[i], -e, jnp.where(at[k], r, e * v[i] - r * v[k])) * over
            n1 = jnp.where(at[k], -a, jnp.where(at[i], r, a * v[k] - r * v[i])) * over
            for j in range(8):
                if j not in (i, k):
                    v[j] = jnp.where(pair[p], 0.0, v[j]) - (n0 * row(v[j], i) + n1 * row(v[j], k))
            v[i], v[k] = -n0, -n1
        if q < last:
            w = tree([v[j] * rows[j] for j in range(8)])
            w = [row(w, j) for j in range(8)]
            for t in range(q + 1, last + 1):
                taken = tree([col(tiles[t], c0 + j) * w[j] for j in range(8)])
                tiles[t] = jnp.where(block, 0.0, tiles[t]) - taken
        forward = strip + tree([jnp.where(sub >= j + 2 - j % 2, u[j], 0.0) * rows[j] for j in range(6)])
        ratio = pr / pa
        second = (forward - ratio * pltpu.roll(forward, 1, 0)) * lax.rsqrt(pe - ratio * pr)
        scaled = jnp.where(odd, second, forward * lax.rsqrt(pa))
        out[c0 : c0 + 8, :] = jnp.where(lane <= c0 + sub, scaled, 0.0)


def split(x):
    a = x.astype(bf16)
    rest = x - a.astype(f32)
    b = rest.astype(bf16)
    return a, b, (rest - b.astype(f32)).astype(bf16)


def product(x, y, transposed=True):
    c = 1 if transposed else 0
    one = lambda a, b: lax.dot_general(a, b, (((1,), (c,)), ((), ())), preferred_element_type=f32)
    two = jnp.concatenate([y[0], y[1]], axis=1 - c)
    n = two.shape[1 - c] // 2
    high, mid = one(x[0], two), one(x[1], two)
    return ((one(x[0], y[2]) + one(x[2], y[0])) + mid[:, n:]) + (mid[:, :n] + high[:, n:]) + high[:, :n]


def at(i):
    return slice(i * B, i * B + B)


def factor_steps(g, slab, x, piv, ls, xs, cs, inv, ones, ready, given):
    eye = lax.broadcasted_iota(jnp.int32, (B, B), 0) == lax.broadcasted_iota(jnp.int32, (B, B), 1)
    blocks = K // B
    three = range(3)
    ones[...] = jnp.ones_like(ones)
    one = ones[...]
    for k in range(blocks):
        rest, done = slice((k + 1) * B, K), slice(0, k * B)
        ready(k)
        if k == 0:
            d = g[at(0), at(0)]
        else:
            column = split(product(split(cs[k * B : K, :]), li))
            for s in three:
                ls[s, k * B : K, at(k - 1)] = column[s]
            lk = [ls[s, at(k), done] for s in three]
        xp = slab[at(k), :]
        if k:
            xp = xp - product(lk, [xs[s, done, :] for s in three], False)
        if k < blocks - 1:
            c = g[rest, at(k)]
            later = g[at(k + 1), at(k + 1)]
            if k:
                c = c - product([ls[s, rest, done] for s in three], lk)
                ln = [ls[s, at(k + 1), done] for s in three]
                later = later - product(ln, ln)
            cs[rest, :] = c
        eliminate(d, inv, one)
        inverse = inv[...]
        li = split(inverse)
        if k < blocks - 1:
            l1 = split(product(split(cs[at(k + 1), :]), li))
            d = later - product(l1, l1)
        solved = product(li, split(xp), False)
        x[at(k), :] = solved * math.sqrt(ROWS)
        if k < blocks - 1:
            solved = split(solved)
            for s in three:
                xs[s, at(k), :] = solved[s]
        diagonal = jnp.sum(jnp.where(eye, inverse, 0.0), axis=0, keepdims=True)
        piv[k : k + 1, :] = -jnp.log(diagonal) - 0.5 * math.log(ROWS)
        given(k)


def place_bands(gall, g):
    for i in range(K // B):
        for j in range(i + 1):
            d = i - j
            chip = (j, j, j, j + 1, j + 2, i + 1, i, i)[d]
            band = d if d <= 4 else 8 - d
            g[at(i), at(j)] = gall[chip % CHIPS, :, at(band)]


def means_of(expo):
    lane = lax.broadcasted_iota(jnp.int32, (B, B), 1)
    upto = jnp.where(lax.broadcasted_iota(jnp.int32, (B, B), 0) <= lane, 1.0, 0.0).astype(f32)
    sums = dot(expo, upto, 1, 0)
    before = jnp.zeros((1, 1), f32)
    parts = []
    for i in range(K // B):
        parts.append(sums[i : i + 1, :] + before)
        before = before + sums[i : i + 1, B - 1 : B]
    place = lax.broadcasted_iota(jnp.int32, (K // B, B), 0) * B + lax.broadcasted_iota(jnp.int32, (K // B, B), 1)
    return jnp.concatenate(parts, axis=0) / (place + 1).astype(f32)


def factor_kernel(
    cuts, gall, slab, start, handed, exponents, running,
    g, x, piv, allp, ls, xs, cs, inv, ones, xss, xrs, vs, vr,
):
    me = lax.axis_index("col")
    c = lax.axis_index("cuts")
    barrier = pltpu.get_barrier_semaphore()
    for o in range(1, cuts):
        pl.semaphore_signal(
            barrier, inc=1, device_id={"cuts": lax.rem(c + o, cuts), "col": me}, device_id_type=MESH
        )

    @pl.when(c > 0)
    def _():
        for i in range(COL):
            pl.semaphore_signal(barrier, inc=1, device_id={"cuts": c - 1, "col": i}, device_id_type=MESH)

    place_bands(gall, g)

    @pl.when(c == 0)
    def _():
        handed[...] = start[...]

    my_cols = pl.ds(pl.multiple_of(me * B, B), B)

    def rows_out(i):
        return remote(
            x.at[pl.ds(i * HALF, HALF)], handed.at[:, my_cols], xss.at[i], xrs.at[me], {"cuts": c + 1, "col": i}
        )

    def ready(k):
        if k == 1:
            pl.semaphore_wait(barrier, jnp.where(c < cuts - 1, cuts - 1 + COL, cuts - 1))

            @pl.when(c < cuts - 1)
            def _():
                rows_out(0).start()
                rows_out(1).start()

    def given(k):
        if k:

            @pl.when(c < cuts - 1)
            def _():
                rows_out(2 * k).start()
                rows_out(2 * k + 1).start()

    factor_steps(g, slab, x, piv, ls, xs, cs, inv, ones, ready, given)

    give = []
    for o in range(1, cuts):
        s = remote(piv, allp.at[c], vs.at[o], vr.at[o], {"cuts": lax.rem(c + o, cuts), "col": me})
        s.start()
        give.append(s)
    allp[c] = piv[...]
    for o in range(1, cuts):
        come = allp.at[lax.rem(c + cuts - o, cuts)]
        remote(come, come, vs.at[o], vr.at[o], {"cuts": lax.rem(c + o, cuts), "col": me}).wait_recv()
    expo = tree([allp[o] for o in range(cuts)]) / (SLICES * cuts)
    means = means_of(expo)
    here = lax.broadcasted_iota(jnp.int32, (K // B, B), 0) == me // 2
    for value, out in ((expo, exponents), (means, running)):
        line = jnp.sum(jnp.where(here, value, 0.0), axis=0, keepdims=True)
        out[...] = jnp.where(me % 2 == 0, line[:, :HALF], line[:, HALF:])

    @pl.when(c > 0)
    def _():
        for j in range(COL):
            come = handed.at[:, pl.ds(j * B, B)]
            remote(come, come, xss.at[j], xrs.at[j], {"cuts": c - 1, "col": j}).wait_recv()

    @pl.when(c < cuts - 1)
    def _():
        for i in range(COL):
            rows_out(i).wait_send()

    for s in give:
        s.wait_send()


def local(cuts, levels, start_basis):
    start = start_basis[0]
    dma = pltpu.SemaphoreType.DMA
    slab, gall = pl.pallas_call(
        gram_kernel,
        out_shape=(jax.ShapeDtypeStruct((K, B), f32), jax.ShapeDtypeStruct((CHIPS, B, BANDS), f32)),
        in_specs=[VMEM] * 2,
        out_specs=(VMEM,) * 2,
        scratch_shapes=[
            pltpu.VMEM((HALF, ROWS), f32),
            pltpu.VMEM((5, B, SITES), f32),
            pltpu.VMEM((B, BANDS), f32),
            pltpu.VMEM((HALF, BANDS), f32),
            dma((5,)), dma((10,)), dma((4,)), dma((COL,)), dma((COL,)),
            dma, dma, dma((9,)), dma((9,)), dma((9,)), dma((9,)),
        ],
        compiler_params=pltpu.CompilerParams(
            collective_id=1, has_side_effects=True, vmem_limit_bytes=32 << 20
        ),
        name="gram",
    )(levels, start)
    handed, exponents, running = pl.pallas_call(
        functools.partial(factor_kernel, cuts),
        out_shape=(
            jax.ShapeDtypeStruct((HALF, ROWS), f32),
            jax.ShapeDtypeStruct((1, HALF), f32),
            jax.ShapeDtypeStruct((1, HALF), f32),
        ),
        in_specs=[VMEM] * 3,
        out_specs=(VMEM,) * 3,
        scratch_shapes=[
            pltpu.VMEM((K, K), f32),
            pltpu.VMEM((K, B), f32),
            pltpu.VMEM((K // B, B), f32),
            pltpu.VMEM((cuts, K // B, B), f32),
            pltpu.VMEM((3, K, K), bf16),
            pltpu.VMEM((3, K, B), bf16),
            pltpu.VMEM((K, B), f32),
            pltpu.VMEM((B, B), f32),
            pltpu.VMEM((8, B), f32),
            dma((COL,)), dma((COL,)), dma((cuts,)), dma((cuts,)),
        ],
        compiler_params=pltpu.CompilerParams(
            collective_id=2, has_side_effects=True, vmem_limit_bytes=40 << 20
        ),
        name="factor",
    )(gall, slab, start)
    return exponents[0], running[0], handed[None]


def solution(mesh):
    in_specs = (P("cuts", None), P("cuts", "col", None))
    out_specs = (P("col"), P("col"), P("cuts", "col", None))
    return jax.shard_map(
        functools.partial(local, mesh.shape["cuts"]), mesh=mesh, in_specs=in_specs, out_specs=out_specs, check_vma=False
    )
```

```python
import functools
import math

import jax
import jax.numpy as jnp
from jax import lax
from jax.experimental import pallas as pl
from jax.experimental.pallas import tpu as pltpu
from jax.sharding import PartitionSpec as P

M = 32
SITES = 1024
ROWS = 2048
SLICES = 2
B = 128
HALF = 64
CHIPS = 8
COL = 16
K = 1024
BANDS = 6 * B
LAG = 4
WAIT = 2

energy = 0.5
disorder = 4.0
level_span = 65536.0

MESH = pl.DeviceIdType.MESH
VMEM = pl.BlockSpec(memory_space=pltpu.VMEM)
f32 = jnp.float32
bf16 = jnp.bfloat16


def dot(a, b, ca, cb):
    return lax.dot_general(
        a, b, (((ca,), (cb,)), ((), ())), precision=lax.Precision.HIGHEST, preferred_element_type=f32
    )


def remote(src, dst, send, recv, device):
    return pltpu.make_async_remote_copy(
        src_ref=src, dst_ref=dst, send_sem=send, recv_sem=recv, device_id=device, device_id_type=MESH
    )


def neighbours(x):
    site = lax.broadcasted_iota(jnp.int32, x.shape, 1)
    b = lax.rem(site, M)
    around = lambda by: pltpu.roll(x, by % SITES, 1)
    along = jnp.where(b == 0, around(1 - M), around(1)) + jnp.where(b == M - 1, around(M - 1), around(-1))
    return along + around(M) + around(-M)


def tree(terms):
    while len(terms) > 1:
        pairs = [terms[i] + terms[i + 1] for i in range(0, len(terms) - 1, 2)]
        terms = pairs + terms[len(pairs) * 2 :]
    return terms[0]


def eliminate(d, out, one):
    tiles = [d[8 * t : 8 * t + 8, :] for t in range(B // 8)]
    last = len(tiles) - 1
    lane = lax.broadcasted_iota(jnp.int32, (8, B), 1)
    sub = lax.broadcasted_iota(jnp.int32, (8, B), 0)
    row = lambda v, i: jnp.broadcast_to(v[i : i + 1, :], (8, B))
    col = lambda v, c: jnp.broadcast_to(v[:, c : c + 1], (8, B))
    at = [sub == i for i in range(8)]
    pair = [jnp.logical_or(at[i], at[i + 1]) for i in range(0, 8, 2)]
    odd = sub % 2 == 1
    for q in range(last + 1):
        c0 = 8 * q
        block = jnp.logical_and(lane >= c0, lane < c0 + 8)
        v = [col(tiles[q], c0 + j) * one for j in range(8)]
        strip = jnp.where(block, jnp.where(lane - c0 == sub, 1.0, 0.0), tiles[q])
        rows = [row(strip, j) for j in range(8)]
        u = [None] * 8
        for p in range(4):
            i, k = 2 * p, 2 * p + 1
            a, r, e = row(v[i], i), row(v[i], k), row(v[k], k)
            over = 1.0 / (a * e - r * r)
            for j in range(i):
                u[j] = v[j] if u[j] is None else jnp.where(pair[p], v[j], u[j])
            if p == 0:
                pa, pr, pe = a, r, e
            else:
                pa, pr, pe = (jnp.where(pair[p], x, y) for x, y in ((a, pa), (r, pr), (e, pe)))
            if q == last and p == 3:
                break
            n0 = jnp.where(at[i], -e, jnp.where(at[k], r, e * v[i] - r * v[k])) * over
            n1 = jnp.where(at[k], -a, jnp.where(at[i], r, a * v[k] - r * v[i])) * over
            for j in range(8):
                if j not in (i, k):
                    v[j] = jnp.where(pair[p], 0.0, v[j]) - (n0 * row(v[j], i) + n1 * row(v[j], k))
            v[i], v[k] = -n0, -n1
        if q < last:
            w = tree([v[j] * rows[j] for j in range(8)])
            w = [row(w, j) for j in range(8)]
            for t in range(q + 1, last + 1):
                taken = tree([col(tiles[t], c0 + j) * w[j] for j in range(8)])
                tiles[t] = jnp.where(block, 0.0, tiles[t]) - taken
        forward = strip + tree([jnp.where(sub >= j + 2 - j % 2, u[j], 0.0) * rows[j] for j in range(6)])
        ratio = pr / pa
        second = (forward - ratio * pltpu.roll(forward, 1, 0)) * lax.rsqrt(pe - ratio * pr)
        scaled = jnp.where(odd, second, forward * lax.rsqrt(pa))
        out[c0 : c0 + 8, :] = jnp.where(lane <= c0 + sub, scaled, 0.0)


def split(x):
    a = x.astype(bf16)
    rest = x - a.astype(f32)
    b = rest.astype(bf16)
    return a, b, (rest - b.astype(f32)).astype(bf16)


def product(x, y, transposed=True):
    c = 1 if transposed else 0
    one = lambda a, b: lax.dot_general(a, b, (((1,), (c,)), ((), ())), preferred_element_type=f32)
    two = jnp.concatenate([y[0], y[1]], axis=1 - c)
    n = two.shape[1 - c] // 2
    high, mid = one(x[0], two), one(x[1], two)
    return ((one(x[0], y[2]) + one(x[2], y[0])) + mid[:, n:]) + (mid[:, :n] + high[:, n:]) + high[:, :n]


def at(i):
    return slice(i * B, i * B + B)


def means_of(expo):
    lane = lax.broadcasted_iota(jnp.int32, (B, B), 1)
    upto = jnp.where(lax.broadcasted_iota(jnp.int32, (B, B), 0) <= lane, 1.0, 0.0).astype(f32)
    sums = dot(expo, upto, 1, 0)
    before = jnp.zeros((1, 1), f32)
    parts = []
    for i in range(K // B):
        parts.append(sums[i : i + 1, :] + before)
        before = before + sums[i : i + 1, B - 1 : B]
    place = lax.broadcasted_iota(jnp.int32, (K // B, B), 0) * B + lax.broadcasted_iota(jnp.int32, (K // B, B), 1)
    return jnp.concatenate(parts, axis=0) / (place + 1).astype(f32)


def sweep_kernel(
    cuts, lev, start, handed, exponents, running,
    prop, gat, part, other, first, near, far, across, slab, x, piv, allp, ls, xs, cs, lis, inv, ones,
    gs, gr, fs, g2r, ps, pr, d0s, d0r, ns, nr, nis, nir, f3s, f3r, f3is, f3ir, f4s, f4r, f4is, f4ir,
    als, alr, xss, xrs, vs, vr,
):
    me = lax.axis_index("col")
    c = lax.axis_index("cuts")
    z, h = me // 2, me % 2
    up, down = lax.rem(z + 1, CHIPS), lax.rem(z + CHIPS - 1, CHIPS)
    partner = z * 2 + 1 - h
    mine = pl.ds(pl.multiple_of(h * HALF, HALF), HALF)
    theirs = pl.ds(pl.multiple_of((1 - h) * HALF, HALF), HALF)
    my_cols = pl.ds(pl.multiple_of(me * B, B), B)
    my_rows = pl.ds(pl.multiple_of(me * HALF, HALF), HALF)
    blocks = K // B
    sends = []

    barrier = pltpu.get_barrier_semaphore()
    for o in range(1, COL):
        pl.semaphore_signal(barrier, inc=1, device_id={"col": lax.rem(me + o, COL)}, device_id_type=MESH)
    for o in range(1, cuts):
        pl.semaphore_signal(
            barrier, inc=1, device_id={"cuts": lax.rem(c + o, cuts), "col": me}, device_id_type=MESH
        )

    @pl.when(c > 0)
    def _():
        for i in range(COL):
            pl.semaphore_signal(barrier, inc=1, device_id={"cuts": c - 1, "col": i}, device_id_type=MESH)

    upper = start[:, :SITES]
    lower = start[:, SITES:]
    for n in range(SLICES):
        onsite = disorder * (lev[n : n + 1, :].astype(f32) / level_span - 0.5)
        upper, lower = (energy - onsite) * upper - neighbours(upper) - lower, upper
    prop[:, :SITES] = upper
    prop[:, SITES:] = lower

    @pl.when(c == 0)
    def _():
        handed[...] = start[...]

    everyone = COL - 1 + cuts - 1
    pl.semaphore_wait(barrier, jnp.where(c < cuts - 1, everyone + COL, everyone))

    their_half = pl.ds(pl.multiple_of((1 - h) * SITES, SITES), SITES)
    swap = remote(prop.at[:, their_half], gat.at[0, mine], gs.at[4], gr.at[h], {"col": partner})
    swap.start()
    sends.append(swap)
    for way in range(2):
        for t, (slot, chip) in enumerate(((1, up), (3, down))):
            f = h if way == 0 else 1 - h
            half = prop.at[:, pl.ds(pl.multiple_of(f * SITES, SITES), SITES)]
            out = remote(half, gat.at[slot, mine], gs.at[2 * way + t], gr.at[2 * slot + h], {"col": chip * 2 + f})
            out.start()
            sends.append(out)
    gat[0, mine, :] = prop[:, pl.ds(pl.multiple_of(h * SITES, SITES), SITES)]

    def come(ref, sem):
        remote(ref, ref, gs.at[0], sem, {"col": partner}).wait_recv()

    def arrived(slot, s):
        come(gat.at[slot, pl.ds(pl.multiple_of(s * HALF, HALF), HALF)], gr.at[2 * slot + s])

    kinds = ((0, 0, 0, 0), (0, 1, 0, 3), (-1, 2, 1, 3), (-1, 3, 1, 4), (-2, 3, 2, 3), (-2, 4, 2, 4))

    def make(kind):
        offset, d, one, two = kinds[kind]
        if d == 0:
            value = dot(gat[one], gat[one], 1, 1)
        else:
            wraps = lax.rem(z + CHIPS + offset, CHIPS) + d >= CHIPS
            value = dot(gat[jnp.where(wraps, one, two)], gat[jnp.where(wraps, two, one)], 1, 1)
        part[:, kind * B : kind * B + B] = value

    def pair_sum(group, lo, hi):
        cols = pl.ds(lo * B, (hi - lo) * B)
        both = remote(part.at[theirs, cols], other.at[:, cols], ps.at[group], pr.at[group], {"col": partner})
        both.start()
        both.wait_recv()
        sends.append(both)
        return part[mine, lo * B : hi * B] + other[:, lo * B : hi * B]

    quarter = HALF // 2
    halves = [pl.ds(pl.multiple_of(h * HALF + q * quarter, quarter), quarter) for q in range(2)]
    their_halves = [pl.ds(pl.multiple_of((1 - h) * HALF + q * quarter, quarter), quarter) for q in range(2)]

    def near_step(d):
        rows = (mine, mine) if d < 4 else halves
        for way, (chip, to) in enumerate(
            ((lax.rem(z + CHIPS - d + 1, CHIPS), up), (lax.rem(z + d - 1, CHIPS), down))
        ):
            ref = near.at[chip, rows[way]]
            out = remote(ref, ref, ns.at[2 * d + way], nr.at[2 * d + way], {"col": to * 2 + h})
            out.start()
            sends.append(out)

    def near_inside(chip, rows, i):
        ref = near.at[chip, rows]
        out = remote(ref, ref, nis.at[i], nir.at[i], {"col": partner})
        out.start()
        sends.append(out)

    def near_chips(d):
        return lax.rem(z + CHIPS - d, CHIPS), lax.rem(z + d, CHIPS)

    def near_come(d):
        rows = (mine, mine) if d < 4 else halves
        for way, chip in enumerate(near_chips(d)):
            come(near.at[chip, rows[way]], nr.at[2 * d + way])
            near_inside(chip, rows[way], 2 * d + way)

    def far_place(way):
        return lax.rem(z + CHIPS - way, CHIPS)

    def far_out(way, o):
        ref = far.at[far_place(way), mine]
        to = lax.rem(z + (o if way else CHIPS - o), CHIPS)
        return remote(ref, ref, f3s.at[4 * way + o], f3r.at[4 * way + o], {"col": to * 2 + h})

    def far_from(way, o):
        return lax.rem(z + (CHIPS - o - 1 if way else o), CHIPS)

    def far_inside(way, o):
        ref = far.at[far_from(way, o), mine]
        return remote(ref, ref, f3is.at[4 * way + o], f3ir.at[4 * way + o], {"col": partner})

    steps4 = (1, CHIPS - 1, 2 + 4 * h)

    def across_of(chip):
        return lax.rem(chip + CHIPS - 2, CHIPS // 2)

    def across_out(i):
        ref = across.at[across_of(z), mine]
        return remote(ref, ref, f4s.at[i], f4r.at[i], {"col": lax.rem(z + steps4[i], CHIPS) * 2 + h})

    def across_from(i):
        return across_of(z) if i == 3 else across_of(lax.rem(z + CHIPS - steps4[i], CHIPS))

    def across_inside(i):
        ref = across.at[across_from(i), mine]
        return remote(ref, ref, f4is.at[i], f4ir.at[i], {"col": partner})

    def piece(n):
        s = h if n < 2 else 1 - h
        return pl.ds(pl.multiple_of(s * HALF + n % 2 * quarter, quarter), quarter)

    def second_hop(n):
        for way, (slot, chip) in enumerate(((1, up), (3, down))):
            out = remote(
                gat.at[slot, piece(n)], gat.at[slot + 1, piece(n)], fs.at[4 * way + n], g2r.at[4 * way + n],
                {"col": chip * 2 + h},
            )
            out.start()
            sends.append(out)

    def far_issue():
        for n in range(4):
            for way in range(2):
                come(gat.at[2 * way + 2, piece(n)], g2r.at[4 * way + n])
        make(3)
        make(4)
        make(5)
        late = pair_sum(2, 3, 6)
        far[far_place(0), mine, :] = late[:, :B]
        far[far_place(1), mine, :] = late[:, B : 2 * B]
        across[across_of(z), mine, :] = late[:, 2 * B :]
        for o in range(1, 4):
            far_out(0, o).start()
            far_out(1, o).start()
            if o < 3:
                across_out(o - 1).start()
        across_out(2).start()
        far_inside(0, 0).start()
        far_inside(1, 0).start()
        across_inside(3).start()

    def far_finish():
        for o in range(1, 4):
            for way in range(2):
                come(far.at[far_from(way, o), mine], f3r.at[4 * way + o])
                far_inside(way, o).start()
        for i in range(3):
            come(across.at[across_from(i), mine], f4r.at[i])
            across_inside(i).start()

    def far_complete():
        for o in range(4):
            for way in range(2):
                come(far.at[far_from(way, o), theirs], f3ir.at[4 * way + o])
        for i in range(4):
            n = across_of(z) if i == 3 else across_of(lax.rem(z + CHIPS - (1, CHIPS - 1, 6 - 4 * h)[i], CHIPS))
            come(across.at[n, theirs], f4ir.at[i])

    def columns_issue():
        for o in range(1, COL):
            out = columns_out(o)
            out.start()
            sends.append(out)
        slab[my_rows, :] = prop[:, my_cols]

    def gram_block(i, j):
        d = i - j
        if d <= 2 or d >= 6:
            chip, kind = (j, j, j + 1, 0, 0, 0, i + 1, i)[d], min(d, CHIPS - d)
            return near[chip % CHIPS, :, at(kind)]
        if d == 4:
            return across[j]
        return far[((j if d == 3 else i) + 1) % CHIPS]

    def columns_out(o):
        d = lax.rem(me + o, COL)
        cols = pl.ds(pl.multiple_of(d * B, B), B)
        return remote(prop.at[:, cols], slab.at[my_rows], als.at[o], alr.at[o], {"col": d})

    def rows_out(i):
        return remote(
            x.at[pl.ds(i * HALF, HALF)], handed.at[:, my_cols], xss.at[i], xrs.at[me], {"cuts": c + 1, "col": i}
        )

    come(gat.at[0, theirs], gr.at[1 - h])
    make(0)

    def first_out(o):
        ref = first.at[mine]
        return remote(ref, ref, d0s.at[o], d0r.at[h], {"col": lax.rem(me + o, COL)})

    diagonal_half = pair_sum(0, 0, 1)
    near[z, mine, 0:B] = diagonal_half

    @pl.when(z == 0)
    def _():
        first[mine, :] = diagonal_half
        for o in range(1, COL):
            first_out(o).start()

    arrived(1, h)
    arrived(3, h)
    second_hop(0)
    arrived(1, 1 - h)
    arrived(3, 1 - h)
    make(1)
    make(2)
    near[z, mine, B : 3 * B] = pair_sum(1, 1, 3)
    near_step(1)
    second_hop(1)
    near_inside(z, mine, 0)
    near_come(1)
    near_step(2)
    second_hop(2)

    @pl.when(z == 0)
    def _():
        come(first.at[theirs], d0r.at[1 - h])

    @pl.when(z > 0)
    def _():
        for s in range(2):
            come(first.at[pl.ds(s * HALF, HALF)], d0r.at[s])

    ones[...] = jnp.ones_like(ones)
    one = ones[...]
    eliminate(first[...], inv, one)

    near_come(2)
    near_step(3)
    second_hop(3)
    near_come(3)
    near_step(4)
    far_issue()
    columns_issue()
    near_come(4)
    for d in range(5):
        rows = (theirs, theirs) if d < 4 else their_halves
        for way, chip in enumerate(near_chips(d)):
            if d or way == 0:
                come(near.at[chip, rows[way]], nir.at[2 * d + way])

    eye = lax.broadcasted_iota(jnp.int32, (B, B), 0) == lax.broadcasted_iota(jnp.int32, (B, B), 1)
    three = range(3)

    def known(k):
        done = slice(0, k * B)
        xp = slab[at(k), :]
        if k:
            xp = xp - product([ls[s, at(k), done] for s in three], [xs[s, done, :] for s in three], False)
        return xp

    def solve(k, xp, inverse):
        solved = product(inverse, split(xp), False)
        x[at(k), :] = solved * math.sqrt(ROWS)
        if k < blocks - 1:
            solved = split(solved)
            for s in three:
                xs[s, at(k), :] = solved[s]

    def hand_over(ks):
        @pl.when(c < cuts - 1)
        def _():
            for k in ks:
                rows_out(2 * k).start()
                rows_out(2 * k + 1).start()

    for k in range(blocks):
        done = slice(0, k * B)
        top = WAIT + 1 if k < WAIT else blocks
        rest = slice((k + 1) * B, top * B)
        if k == WAIT:
            far_finish()
            far_complete()
        if k == LAG:
            for o in range(1, COL):
                rows = pl.ds(pl.multiple_of(lax.rem(me + COL - o, COL) * HALF, HALF), HALF)
                come(slab.at[rows], alr.at[o])
        if k:
            before = (WAIT + 1 if k <= WAIT else blocks) * B
            column = split(product(split(cs[k * B : before, :]), li))
            for s in three:
                ls[s, k * B : before, at(k - 1)] = column[s]
        if k == WAIT:
            low = slice((WAIT + 1) * B, K)
            for j in range(WAIT):
                early = slice(0, j * B)
                column = jnp.concatenate([gram_block(i, j) for i in range(WAIT + 1, blocks)], axis=0)
                if j:
                    column = column - product([ls[s, low, early] for s in three], [ls[s, at(j), early] for s in three])
                column = split(product(split(column), [lis[s, j] for s in three]))
                for s in three:
                    ls[s, low, at(j)] = column[s]
        if k:
            lk = [ls[s, at(k), done] for s in three]
        if k == LAG:
            for j in range(k):
                solve(j, known(j), [lis[s, j] for s in three])
        if k >= LAG:
            xp = known(k)
        if k < blocks - 1:
            later = gram_block(k + 1, k + 1)
            if k:
                taken = product([ls[s, rest, done] for s in three], lk)
                for i in range(k + 1, top):
                    cs[at(i), :] = gram_block(i, k) - taken[at(i - k - 1), :]
            else:
                for i in range(1, top):
                    cs[at(i), :] = gram_block(i, 0)
            if k:
                ln = [ls[s, at(k + 1), done] for s in three]
                later = later - product(ln, ln)
        if k:
            eliminate(d, inv, one)
        inverse = inv[...]
        li = split(inverse)
        if k < blocks - 1:
            l1 = split(product(split(cs[at(k + 1), :]), li))
            d = later - product(l1, l1)
        if k >= LAG:
            solve(k, xp, li)
        else:
            for s in three:
                lis[s, k] = li[s]
        diagonal = jnp.sum(jnp.where(eye, inverse, 0.0), axis=0, keepdims=True)
        piv[k : k + 1, :] = -jnp.log(diagonal) - 0.5 * math.log(ROWS)
        if k >= LAG:
            hand_over(range(k + 1) if k == LAG else (k,))

    give = []
    for o in range(1, cuts):
        s = remote(piv, allp.at[c], vs.at[o], vr.at[o], {"cuts": lax.rem(c + o, cuts), "col": me})
        s.start()
        give.append(s)
    allp[c] = piv[...]
    for o in range(1, cuts):
        come(allp.at[lax.rem(c + cuts - o, cuts)], vr.at[o])
    expo = tree([allp[o] for o in range(cuts)]) / (SLICES * cuts)
    means = means_of(expo)
    here = lax.broadcasted_iota(jnp.int32, (K // B, B), 0) == z
    for value, out in ((expo, exponents), (means, running)):
        line = jnp.sum(jnp.where(here, value, 0.0), axis=0, keepdims=True)
        out[...] = jnp.where(h == 0, line[:, :HALF], line[:, HALF:])

    @pl.when(c > 0)
    def _():
        for j in range(COL):
            come(handed.at[:, pl.ds(j * B, B)], xrs.at[j])

    @pl.when(c < cuts - 1)
    def _():
        for i in range(COL):
            rows_out(i).wait_send()

    @pl.when(z == 0)
    def _():
        for o in range(1, COL):
            first_out(o).wait_send()

    for way in range(2):
        for o in range(4):
            if o:
                far_out(way, o).wait_send()
            far_inside(way, o).wait_send()
    for i in range(4):
        if i < 3:
            across_out(i).wait_send()
        across_inside(i).wait_send()
    for s in sends + give:
        s.wait_send()


def local(cuts, levels, start_basis):
    start = start_basis[0]
    dma = pltpu.SemaphoreType.DMA
    handed, exponents, running = pl.pallas_call(
        functools.partial(sweep_kernel, cuts),
        out_shape=(
            jax.ShapeDtypeStruct((HALF, ROWS), f32),
            jax.ShapeDtypeStruct((1, HALF), f32),
            jax.ShapeDtypeStruct((1, HALF), f32),
        ),
        in_specs=[VMEM] * 2,
        out_specs=(VMEM,) * 3,
        scratch_shapes=[
            pltpu.VMEM((HALF, ROWS), f32),
            pltpu.VMEM((5, B, SITES), f32),
            pltpu.VMEM((B, BANDS), f32),
            pltpu.VMEM((HALF, BANDS), f32),
            pltpu.VMEM((B, B), f32),
            pltpu.VMEM((CHIPS, B, 3 * B), f32),
            pltpu.VMEM((CHIPS, B, B), f32),
            pltpu.VMEM((CHIPS // 2, B, B), f32),
            pltpu.VMEM((K, B), f32),
            pltpu.VMEM((K, B), f32),
            pltpu.VMEM((K // B, B), f32),
            pltpu.VMEM((cuts, K // B, B), f32),
            pltpu.VMEM((3, K, K), bf16),
            pltpu.VMEM((3, K, B), bf16),
            pltpu.VMEM((K, B), f32),
            pltpu.VMEM((3, max(LAG, 1), B, B), bf16),
            pltpu.VMEM((B, B), f32),
            pltpu.VMEM((8, B), f32),
            dma((5,)), dma((10,)), dma((8,)), dma((8,)), dma((3,)), dma((3,)), dma((COL,)), dma((2,)),
            dma((10,)), dma((10,)), dma((10,)), dma((10,)),
            dma((CHIPS,)), dma((CHIPS,)), dma((CHIPS,)), dma((CHIPS,)), dma((3,)), dma((3,)), dma((4,)), dma((4,)),
            dma((COL,)), dma((COL,)), dma((COL,)), dma((COL,)), dma((cuts,)), dma((cuts,)),
        ],
        compiler_params=pltpu.CompilerParams(
            collective_id=1, has_side_effects=True, vmem_limit_bytes=48 << 20
        ),
        name="sweep",
    )(levels, start)
    return exponents[0], running[0], handed[None]


def solution(mesh):
    in_specs = (P("cuts", None), P("cuts", "col", None))
    out_specs = (P("col"), P("col"), P("cuts", "col", None))
    return jax.shard_map(
        functools.partial(local, mesh.shape["cuts"]), mesh=mesh, in_specs=in_specs, out_specs=out_specs, check_vma=False
    )
```

```python
import functools
import math

import jax
import jax.numpy as jnp
from jax import lax
from jax.experimental import pallas as pl
from jax.experimental.pallas import tpu as pltpu
from jax.sharding import PartitionSpec as P

M = 32
SITES = 1024
ROWS = 2048
SLICES = 2
B = 128
HALF = 64
CHIPS = 8
COL = 16
K = 1024
BANDS = 6 * B
LAG = 4
WAIT = 2

energy = 0.5
disorder = 4.0
level_span = 65536.0

MESH = pl.DeviceIdType.MESH
VMEM = pl.BlockSpec(memory_space=pltpu.VMEM)
f32 = jnp.float32
bf16 = jnp.bfloat16


def dot(a, b, ca, cb):
    return lax.dot_general(
        a, b, (((ca,), (cb,)), ((), ())), precision=lax.Precision.HIGHEST, preferred_element_type=f32
    )


def remote(src, dst, send, recv, device):
    return pltpu.make_async_remote_copy(
        src_ref=src, dst_ref=dst, send_sem=send, recv_sem=recv, device_id=device, device_id_type=MESH
    )


def neighbours(x):
    site = lax.broadcasted_iota(jnp.int32, x.shape, 1)
    b = lax.rem(site, M)
    around = lambda by: pltpu.roll(x, by % SITES, 1)
    along = jnp.where(b == 0, around(1 - M), around(1)) + jnp.where(b == M - 1, around(M - 1), around(-1))
    return along + around(M) + around(-M)


def tree(terms):
    while len(terms) > 1:
        pairs = [terms[i] + terms[i + 1] for i in range(0, len(terms) - 1, 2)]
        terms = pairs + terms[len(pairs) * 2 :]
    return terms[0]


def eliminate(d, out, one):
    tiles = [d[8 * t : 8 * t + 8, :] for t in range(B // 8)]
    last = len(tiles) - 1
    lane = lax.broadcasted_iota(jnp.int32, (8, B), 1)
    sub = lax.broadcasted_iota(jnp.int32, (8, B), 0)
    row = lambda v, i: jnp.broadcast_to(v[i : i + 1, :], (8, B))
    col = lambda v, c: jnp.broadcast_to(v[:, c : c + 1], (8, B))
    at = [sub == i for i in range(8)]
    pair = [jnp.logical_or(at[i], at[i + 1]) for i in range(0, 8, 2)]
    odd = sub % 2 == 1
    for q in range(last + 1):
        c0 = 8 * q
        block = jnp.logical_and(lane >= c0, lane < c0 + 8)
        v = [col(tiles[q], c0 + j) * one for j in range(8)]
        strip = jnp.where(block, jnp.where(lane - c0 == sub, 1.0, 0.0), tiles[q])
        rows = [row(strip, j) for j in range(8)]
        u = [None] * 8
        for p in range(4):
            i, k = 2 * p, 2 * p + 1
            a, r, e = row(v[i], i), row(v[i], k), row(v[k], k)
            over = 1.0 / (a * e - r * r)
            for j in range(i):
                u[j] = v[j] if u[j] is None else jnp.where(pair[p], v[j], u[j])
            if p == 0:
                pa, pr, pe = a, r, e
            else:
                pa, pr, pe = (jnp.where(pair[p], x, y) for x, y in ((a, pa), (r, pr), (e, pe)))
            if q == last and p == 3:
                break
            n0 = jnp.where(at[i], -e, jnp.where(at[k], r, e * v[i] - r * v[k])) * over
            n1 = jnp.where(at[k], -a, jnp.where(at[i], r, a * v[k] - r * v[i])) * over
            for j in range(8):
                if j not in (i, k):
                    v[j] = jnp.where(pair[p], 0.0, v[j]) - (n0 * row(v[j], i) + n1 * row(v[j], k))
            v[i], v[k] = -n0, -n1
        if q < last:
            w = tree([v[j] * rows[j] for j in range(8)])
            w = [row(w, j) for j in range(8)]
            for t in range(q + 1, last + 1):
                taken = tree([col(tiles[t], c0 + j) * w[j] for j in range(8)])
                tiles[t] = jnp.where(block, 0.0, tiles[t]) - taken
        forward = strip + tree([jnp.where(sub >= j + 2 - j % 2, u[j], 0.0) * rows[j] for j in range(6)])
        ratio = pr / pa
        second = (forward - ratio * pltpu.roll(forward, 1, 0)) * lax.rsqrt(pe - ratio * pr)
        scaled = jnp.where(odd, second, forward * lax.rsqrt(pa))
        out[c0 : c0 + 8, :] = jnp.where(lane <= c0 + sub, scaled, 0.0)


def split(x):
    a = x.astype(bf16)
    rest = x - a.astype(f32)
    b = rest.astype(bf16)
    return a, b, (rest - b.astype(f32)).astype(bf16)


def product(x, y, transposed=True):
    c = 1 if transposed else 0
    one = lambda a, b: lax.dot_general(a, b, (((1,), (c,)), ((), ())), preferred_element_type=f32)
    two = jnp.concatenate([y[0], y[1]], axis=1 - c)
    n = two.shape[1 - c] // 2
    high, mid = one(x[0], two), one(x[1], two)
    return ((one(x[0], y[2]) + one(x[2], y[0])) + mid[:, n:]) + (mid[:, :n] + high[:, n:]) + high[:, :n]


def at(i):
    return slice(i * B, i * B + B)


def means_of(expo):
    lane = lax.broadcasted_iota(jnp.int32, (B, B), 1)
    upto = jnp.where(lax.broadcasted_iota(jnp.int32, (B, B), 0) <= lane, 1.0, 0.0).astype(f32)
    sums = dot(expo, upto, 1, 0)
    before = jnp.zeros((1, 1), f32)
    parts = []
    for i in range(K // B):
        parts.append(sums[i : i + 1, :] + before)
        before = before + sums[i : i + 1, B - 1 : B]
    place = lax.broadcasted_iota(jnp.int32, (K // B, B), 0) * B + lax.broadcasted_iota(jnp.int32, (K // B, B), 1)
    return jnp.concatenate(parts, axis=0) / (place + 1).astype(f32)


def sweep_kernel(
    cuts, levels, basis, handed, exponents, running,
    lev, start, ins, prop, gat, part, other, near, far, across, slab, x, piv, allp, ls, xs, cs, lis, inv, ones,
    gs, gr, fs, g2r, ps, pr, ns, nr, nis, nir, f3s, f3r, f3is, f3ir, f4s, f4r, f4is, f4ir,
    als, alr, xss, xrs, vs, vr,
):
    me = lax.axis_index("col")
    c = lax.axis_index("cuts")
    z, h = me // 2, me % 2
    up, down = lax.rem(z + 1, CHIPS), lax.rem(z + CHIPS - 1, CHIPS)
    partner = z * 2 + 1 - h
    mine = pl.ds(pl.multiple_of(h * HALF, HALF), HALF)
    theirs = pl.ds(pl.multiple_of((1 - h) * HALF, HALF), HALF)
    my_cols = pl.ds(pl.multiple_of(me * B, B), B)
    my_rows = pl.ds(pl.multiple_of(me * HALF, HALF), HALF)
    blocks = K // B
    sends = []
    loads = [pltpu.make_async_copy(levels, lev, ins.at[0]), pltpu.make_async_copy(basis, start, ins.at[1])]
    for load in loads:
        load.start()

    barrier = pltpu.get_barrier_semaphore()
    for o in range(1, COL):
        pl.semaphore_signal(barrier, inc=1, device_id={"col": lax.rem(me + o, COL)}, device_id_type=MESH)
    for o in range(1, cuts):
        pl.semaphore_signal(
            barrier, inc=1, device_id={"cuts": lax.rem(c + o, cuts), "col": me}, device_id_type=MESH
        )

    @pl.when(c > 0)
    def _():
        for i in range(COL):
            pl.semaphore_signal(barrier, inc=1, device_id={"cuts": c - 1, "col": i}, device_id_type=MESH)

    for load in loads:
        load.wait()
    upper = start[:, :SITES]
    lower = start[:, SITES:]
    for n in range(SLICES):
        onsite = disorder * (lev[n : n + 1, :].astype(f32) / level_span - 0.5)
        upper, lower = (energy - onsite) * upper - neighbours(upper) - lower, upper
    prop[:, :SITES] = upper
    prop[:, SITES:] = lower

    @pl.when(c == 0)
    def _():
        handed[...] = start[...]

    everyone = COL - 1 + cuts - 1
    pl.semaphore_wait(barrier, jnp.where(c < cuts - 1, everyone + COL, everyone))

    their_half = pl.ds(pl.multiple_of((1 - h) * SITES, SITES), SITES)
    swap = remote(prop.at[:, their_half], gat.at[0, mine], gs.at[4], gr.at[h], {"col": partner})
    swap.start()
    sends.append(swap)
    for way in range(2):
        for t, (slot, chip) in enumerate(((1, up), (3, down))):
            f = h if way == 0 else 1 - h
            half = prop.at[:, pl.ds(pl.multiple_of(f * SITES, SITES), SITES)]
            out = remote(half, gat.at[slot, mine], gs.at[2 * way + t], gr.at[2 * slot + h], {"col": chip * 2 + f})
            out.start()
            sends.append(out)
    gat[0, mine, :] = prop[:, pl.ds(pl.multiple_of(h * SITES, SITES), SITES)]

    def come(ref, sem):
        remote(ref, ref, gs.at[0], sem, {"col": partner}).wait_recv()

    def arrived(slot, s):
        come(gat.at[slot, pl.ds(pl.multiple_of(s * HALF, HALF), HALF)], gr.at[2 * slot + s])

    kinds = ((0, 0, 0, 0), (0, 1, 0, 3), (-1, 2, 1, 3), (-1, 3, 1, 4), (-2, 3, 2, 3), (-2, 4, 2, 4))

    def make(kind):
        offset, d, one, two = kinds[kind]
        if d == 0:
            value = dot(gat[one], gat[one], 1, 1)
        else:
            wraps = lax.rem(z + CHIPS + offset, CHIPS) + d >= CHIPS
            value = dot(gat[jnp.where(wraps, one, two)], gat[jnp.where(wraps, two, one)], 1, 1)
        part[:, kind * B : kind * B + B] = value

    def pair_sum(group, lo, hi):
        cols = pl.ds(lo * B, (hi - lo) * B)
        both = remote(part.at[theirs, cols], other.at[:, cols], ps.at[group], pr.at[group], {"col": partner})
        both.start()
        both.wait_recv()
        sends.append(both)
        return part[mine, lo * B : hi * B] + other[:, lo * B : hi * B]

    quarter = HALF // 2
    halves = [pl.ds(pl.multiple_of(h * HALF + q * quarter, quarter), quarter) for q in range(2)]
    their_halves = [pl.ds(pl.multiple_of((1 - h) * HALF + q * quarter, quarter), quarter) for q in range(2)]

    def near_step(d):
        rows = (mine, mine) if d < 4 else halves
        for way, (chip, to) in enumerate(
            ((lax.rem(z + CHIPS - d + 1, CHIPS), up), (lax.rem(z + d - 1, CHIPS), down))
        ):
            ref = near.at[chip, rows[way]]
            out = remote(ref, ref, ns.at[2 * d + way], nr.at[2 * d + way], {"col": to * 2 + h})
            out.start()
            sends.append(out)

    def near_inside(chip, rows, i):
        ref = near.at[chip, rows]
        out = remote(ref, ref, nis.at[i], nir.at[i], {"col": partner})
        out.start()
        sends.append(out)

    def near_chips(d):
        return lax.rem(z + CHIPS - d, CHIPS), lax.rem(z + d, CHIPS)

    def near_come(d):
        rows = (mine, mine) if d < 4 else halves
        for way, chip in enumerate(near_chips(d)):
            come(near.at[chip, rows[way]], nr.at[2 * d + way])
            near_inside(chip, rows[way], 2 * d + way)

    def far_place(way):
        return lax.rem(z + CHIPS - way, CHIPS)

    def far_out(way, o):
        ref = far.at[far_place(way), mine]
        to = lax.rem(z + (o if way else CHIPS - o), CHIPS)
        return remote(ref, ref, f3s.at[4 * way + o], f3r.at[4 * way + o], {"col": to * 2 + h})

    def far_from(way, o):
        return lax.rem(z + (CHIPS - o - 1 if way else o), CHIPS)

    def far_inside(way, o):
        ref = far.at[far_from(way, o), mine]
        return remote(ref, ref, f3is.at[4 * way + o], f3ir.at[4 * way + o], {"col": partner})

    steps4 = (1, CHIPS - 1, 2 + 4 * h)

    def across_of(chip):
        return lax.rem(chip + CHIPS - 2, CHIPS // 2)

    def across_out(i):
        ref = across.at[across_of(z), mine]
        return remote(ref, ref, f4s.at[i], f4r.at[i], {"col": lax.rem(z + steps4[i], CHIPS) * 2 + h})

    def across_from(i):
        return across_of(z) if i == 3 else across_of(lax.rem(z + CHIPS - steps4[i], CHIPS))

    def across_inside(i):
        ref = across.at[across_from(i), mine]
        return remote(ref, ref, f4is.at[i], f4ir.at[i], {"col": partner})

    def piece(n):
        s = h if n < 2 else 1 - h
        return pl.ds(pl.multiple_of(s * HALF + n % 2 * quarter, quarter), quarter)

    def second_hop(n):
        for way, (slot, chip) in enumerate(((1, up), (3, down))):
            out = remote(
                gat.at[slot, piece(n)], gat.at[slot + 1, piece(n)], fs.at[4 * way + n], g2r.at[4 * way + n],
                {"col": chip * 2 + h},
            )
            out.start()
            sends.append(out)

    def far_issue():
        for n in range(4):
            for way in range(2):
                come(gat.at[2 * way + 2, piece(n)], g2r.at[4 * way + n])
        make(3)
        make(4)
        make(5)
        late = pair_sum(2, 3, 6)
        far[far_place(0), mine, :] = late[:, :B]
        far[far_place(1), mine, :] = late[:, B : 2 * B]
        across[across_of(z), mine, :] = late[:, 2 * B :]
        for o in range(1, 4):
            far_out(0, o).start()
            far_out(1, o).start()
            if o < 3:
                across_out(o - 1).start()
        across_out(2).start()
        far_inside(0, 0).start()
        far_inside(1, 0).start()
        across_inside(3).start()

    def far_finish():
        for o in range(1, 4):
            for way in range(2):
                come(far.at[far_from(way, o), mine], f3r.at[4 * way + o])
                far_inside(way, o).start()
        for i in range(3):
            come(across.at[across_from(i), mine], f4r.at[i])
            across_inside(i).start()

    def far_complete():
        for o in range(4):
            for way in range(2):
                come(far.at[far_from(way, o), theirs], f3ir.at[4 * way + o])
        for i in range(4):
            n = across_of(z) if i == 3 else across_of(lax.rem(z + CHIPS - (1, CHIPS - 1, 6 - 4 * h)[i], CHIPS))
            come(across.at[n, theirs], f4ir.at[i])

    def columns_issue():
        for o in range(1, COL):
            out = columns_out(o)
            out.start()
            sends.append(out)
        slab[my_rows, :] = prop[:, my_cols]

    def gram_block(i, j):
        d = i - j
        if d <= 2 or d >= 6:
            chip, kind = (j, j, j + 1, 0, 0, 0, i + 1, i)[d], min(d, CHIPS - d)
            return near[chip % CHIPS, :, at(kind)]
        if d == 4:
            return across[j]
        return far[((j if d == 3 else i) + 1) % CHIPS]

    def columns_out(o):
        d = lax.rem(me + o, COL)
        cols = pl.ds(pl.multiple_of(d * B, B), B)
        return remote(prop.at[:, cols], slab.at[my_rows], als.at[o], alr.at[o], {"col": d})

    def rows_out(i):
        return remote(
            x.at[pl.ds(i * HALF, HALF)], handed.at[:, my_cols], xss.at[i], xrs.at[me], {"cuts": c + 1, "col": i}
        )

    come(gat.at[0, theirs], gr.at[1 - h])
    make(0)

    near[z, mine, 0:B] = pair_sum(0, 0, 1)

    arrived(1, h)
    arrived(3, h)
    second_hop(0)
    arrived(1, 1 - h)
    arrived(3, 1 - h)
    make(1)
    make(2)
    near[z, mine, B : 3 * B] = pair_sum(1, 1, 3)
    near_step(1)
    second_hop(1)
    near_inside(z, mine, 0)
    near_come(1)
    near_step(2)
    second_hop(2)

    near_come(2)
    near_step(3)
    second_hop(3)
    near_come(3)
    near_step(4)
    far_issue()
    columns_issue()
    near_come(4)
    for d in range(5):
        rows = (theirs, theirs) if d < 4 else their_halves
        for way, chip in enumerate(near_chips(d)):
            if d or way == 0:
                come(near.at[chip, rows[way]], nir.at[2 * d + way])

    ones[...] = jnp.ones_like(ones)
    one = ones[...]

    eye = lax.broadcasted_iota(jnp.int32, (B, B), 0) == lax.broadcasted_iota(jnp.int32, (B, B), 1)
    three = range(3)

    def known(k):
        done = slice(0, k * B)
        xp = slab[at(k), :]
        if k:
            xp = xp - product([ls[s, at(k), done] for s in three], [xs[s, done, :] for s in three], False)
        return xp

    def solve(k, xp, inverse):
        solved = product(inverse, split(xp), False)
        x[at(k), :] = solved * math.sqrt(ROWS)
        if k < blocks - 1:
            solved = split(solved)
            for s in three:
                xs[s, at(k), :] = solved[s]

    def hand_over(ks):
        @pl.when(c < cuts - 1)
        def _():
            for k in ks:
                rows_out(2 * k).start()
                rows_out(2 * k + 1).start()

    for k in range(blocks):
        done = slice(0, k * B)
        top = WAIT + 1 if k < WAIT else blocks
        rest = slice((k + 1) * B, top * B)
        if k == WAIT:
            far_finish()
            far_complete()
        if k == LAG:
            for o in range(1, COL):
                rows = pl.ds(pl.multiple_of(lax.rem(me + COL - o, COL) * HALF, HALF), HALF)
                come(slab.at[rows], alr.at[o])
        if k:
            before = (WAIT + 1 if k <= WAIT else blocks) * B
            column = split(product(split(cs[k * B : before, :]), li))
            for s in three:
                ls[s, k * B : before, at(k - 1)] = column[s]
        if k == WAIT:
            low = slice((WAIT + 1) * B, K)
            for j in range(WAIT):
                early = slice(0, j * B)
                column = jnp.concatenate([gram_block(i, j) for i in range(WAIT + 1, blocks)], axis=0)
                if j:
                    column = column - product([ls[s, low, early] for s in three], [ls[s, at(j), early] for s in three])
                column = split(product(split(column), [lis[s, j] for s in three]))
                for s in three:
                    ls[s, low, at(j)] = column[s]
        if k:
            lk = [ls[s, at(k), done] for s in three]
        if k == LAG:
            for j in range(k):
                solve(j, known(j), [lis[s, j] for s in three])
        if k >= LAG:
            xp = known(k)
        if k < blocks - 1:
            later = gram_block(k + 1, k + 1)
            if k:
                taken = product([ls[s, rest, done] for s in three], lk)
                for i in range(k + 1, top):
                    cs[at(i), :] = gram_block(i, k) - taken[at(i - k - 1), :]
            else:
                for i in range(1, top):
                    cs[at(i), :] = gram_block(i, 0)
            if k:
                ln = [ls[s, at(k + 1), done] for s in three]
                later = later - product(ln, ln)
        if k == 0:
            d = gram_block(0, 0)
        eliminate(d, inv, one)
        inverse = inv[...]
        li = split(inverse)
        if k < blocks - 1:
            l1 = split(product(split(cs[at(k + 1), :]), li))
            d = later - product(l1, l1)
        if k >= LAG:
            solve(k, xp, li)
        else:
            for s in three:
                lis[s, k] = li[s]
        diagonal = jnp.sum(jnp.where(eye, inverse, 0.0), axis=0, keepdims=True)
        piv[k : k + 1, :] = -jnp.log(diagonal) - 0.5 * math.log(ROWS)
        if k >= LAG:
            hand_over(range(k + 1) if k == LAG else (k,))

    give = []
    for o in range(1, cuts):
        s = remote(piv, allp.at[c], vs.at[o], vr.at[o], {"cuts": lax.rem(c + o, cuts), "col": me})
        s.start()
        give.append(s)
    allp[c] = piv[...]
    for o in range(1, cuts):
        come(allp.at[lax.rem(c + cuts - o, cuts)], vr.at[o])
    expo = tree([allp[o] for o in range(cuts)]) / (SLICES * cuts)
    means = means_of(expo)
    here = lax.broadcasted_iota(jnp.int32, (K // B, B), 0) == z
    for value, out in ((expo, exponents), (means, running)):
        line = jnp.sum(jnp.where(here, value, 0.0), axis=0, keepdims=True)
        out[...] = jnp.where(h == 0, line[:, :HALF], line[:, HALF:])

    @pl.when(c > 0)
    def _():
        for j in range(COL):
            come(handed.at[:, pl.ds(j * B, B)], xrs.at[j])

    @pl.when(c < cuts - 1)
    def _():
        for i in range(COL):
            rows_out(i).wait_send()

    for way in range(2):
        for o in range(4):
            if o:
                far_out(way, o).wait_send()
            far_inside(way, o).wait_send()
    for i in range(4):
        if i < 3:
            across_out(i).wait_send()
        across_inside(i).wait_send()
    for s in sends + give:
        s.wait_send()


def local(cuts, levels, start_basis):
    start = start_basis[0]
    dma = pltpu.SemaphoreType.DMA
    handed, exponents, running = pl.pallas_call(
        functools.partial(sweep_kernel, cuts),
        out_shape=(
            jax.ShapeDtypeStruct((HALF, ROWS), f32),
            jax.ShapeDtypeStruct((1, HALF), f32),
            jax.ShapeDtypeStruct((1, HALF), f32),
        ),
        in_specs=[pl.BlockSpec(memory_space=pl.ANY)] * 2,
        out_specs=(VMEM,) * 3,
        scratch_shapes=[
            pltpu.VMEM((SLICES, SITES), jnp.int32),
            pltpu.VMEM((HALF, ROWS), f32),
            dma((2,)),
            pltpu.VMEM((HALF, ROWS), f32),
            pltpu.VMEM((5, B, SITES), f32),
            pltpu.VMEM((B, BANDS), f32),
            pltpu.VMEM((HALF, BANDS), f32),
            pltpu.VMEM((CHIPS, B, 3 * B), f32),
            pltpu.VMEM((CHIPS, B, B), f32),
            pltpu.VMEM((CHIPS // 2, B, B), f32),
            pltpu.VMEM((K, B), f32),
            pltpu.VMEM((K, B), f32),
            pltpu.VMEM((K // B, B), f32),
            pltpu.VMEM((cuts, K // B, B), f32),
            pltpu.VMEM((3, K, K), bf16),
            pltpu.VMEM((3, K, B), bf16),
            pltpu.VMEM((K, B), f32),
            pltpu.VMEM((3, max(LAG, 1), B, B), bf16),
            pltpu.VMEM((B, B), f32),
            pltpu.VMEM((8, B), f32),
            dma((5,)), dma((10,)), dma((8,)), dma((8,)), dma((3,)), dma((3,)),
            dma((10,)), dma((10,)), dma((10,)), dma((10,)),
            dma((CHIPS,)), dma((CHIPS,)), dma((CHIPS,)), dma((CHIPS,)), dma((3,)), dma((3,)), dma((4,)), dma((4,)),
            dma((COL,)), dma((COL,)), dma((COL,)), dma((COL,)), dma((cuts,)), dma((cuts,)),
        ],
        compiler_params=pltpu.CompilerParams(
            collective_id=1, has_side_effects=True, vmem_limit_bytes=48 << 20
        ),
        name="sweep",
    )(levels, start)
    return exponents[0], running[0], handed[None]


def solution(mesh):
    in_specs = (P("cuts", None), P("cuts", "col", None))
    out_specs = (P("col"), P("col"), P("cuts", "col", None))
    return jax.shard_map(
        functools.partial(local, mesh.shape["cuts"]), mesh=mesh, in_specs=in_specs, out_specs=out_specs, check_vma=False
    )
```

```python
import functools
import math

import jax
import jax.numpy as jnp
from jax import lax
from jax.experimental import pallas as pl
from jax.experimental.pallas import tpu as pltpu
from jax.sharding import PartitionSpec as P

M = 32
SITES = 1024
ROWS = 2048
SLICES = 2
B = 128
HALF = 64
CHIPS = 8
COL = 16
K = 1024
BANDS = 6 * B
LAG = 4
WAIT = 2

energy = 0.5
disorder = 4.0
level_span = 65536.0

MESH = pl.DeviceIdType.MESH
VMEM = pl.BlockSpec(memory_space=pltpu.VMEM)
f32 = jnp.float32
bf16 = jnp.bfloat16


def dot(a, b, ca, cb):
    return lax.dot_general(
        a, b, (((ca,), (cb,)), ((), ())), precision=lax.Precision.HIGHEST, preferred_element_type=f32
    )


def remote(src, dst, send, recv, device):
    return pltpu.make_async_remote_copy(
        src_ref=src, dst_ref=dst, send_sem=send, recv_sem=recv, device_id=device, device_id_type=MESH
    )


def neighbours(x):
    site = lax.broadcasted_iota(jnp.int32, x.shape, 1)
    b = lax.rem(site, M)
    around = lambda by: pltpu.roll(x, by % SITES, 1)
    along = jnp.where(b == 0, around(1 - M), around(1)) + jnp.where(b == M - 1, around(M - 1), around(-1))
    return along + around(M) + around(-M)


def tree(terms):
    while len(terms) > 1:
        pairs = [terms[i] + terms[i + 1] for i in range(0, len(terms) - 1, 2)]
        terms = pairs + terms[len(pairs) * 2 :]
    return terms[0]


def eliminate(d, out, one):
    tiles = [d[8 * t : 8 * t + 8, :] for t in range(B // 8)]
    last = len(tiles) - 1
    lane = lax.broadcasted_iota(jnp.int32, (8, B), 1)
    sub = lax.broadcasted_iota(jnp.int32, (8, B), 0)
    row = lambda v, i: jnp.broadcast_to(v[i : i + 1, :], (8, B))
    col = lambda v, c: jnp.broadcast_to(v[:, c : c + 1], (8, B))
    at = [sub == i for i in range(8)]
    pair = [jnp.logical_or(at[i], at[i + 1]) for i in range(0, 8, 2)]
    odd = sub % 2 == 1
    for q in range(last + 1):
        c0 = 8 * q
        block = jnp.logical_and(lane >= c0, lane < c0 + 8)
        v = [col(tiles[q], c0 + j) * one for j in range(8)]
        strip = jnp.where(block, jnp.where(lane - c0 == sub, 1.0, 0.0), tiles[q])
        rows = [row(strip, j) for j in range(8)]
        u = [None] * 8
        for p in range(4):
            i, k = 2 * p, 2 * p + 1
            a, r, e = row(v[i], i), row(v[i], k), row(v[k], k)
            over = 1.0 / (a * e - r * r)
            for j in range(i):
                u[j] = v[j] if u[j] is None else jnp.where(pair[p], v[j], u[j])
            if p == 0:
                pa, pr, pe = a, r, e
            else:
                pa, pr, pe = (jnp.where(pair[p], x, y) for x, y in ((a, pa), (r, pr), (e, pe)))
            if q == last and p == 3:
                break
            n0 = jnp.where(at[i], -e, jnp.where(at[k], r, e * v[i] - r * v[k])) * over
            n1 = jnp.where(at[k], -a, jnp.where(at[i], r, a * v[k] - r * v[i])) * over
            for j in range(8):
                if j not in (i, k):
                    v[j] = jnp.where(pair[p], 0.0, v[j]) - (n0 * row(v[j], i) + n1 * row(v[j], k))
            v[i], v[k] = -n0, -n1
        if q < last:
            w = tree([v[j] * rows[j] for j in range(8)])
            w = [row(w, j) for j in range(8)]
            for t in range(q + 1, last + 1):
                taken = tree([col(tiles[t], c0 + j) * w[j] for j in range(8)])
                tiles[t] = jnp.where(block, 0.0, tiles[t]) - taken
        forward = strip + tree([jnp.where(sub >= j + 2 - j % 2, u[j], 0.0) * rows[j] for j in range(6)])
        ratio = pr / pa
        second = (forward - ratio * pltpu.roll(forward, 1, 0)) * lax.rsqrt(pe - ratio * pr)
        scaled = jnp.where(odd, second, forward * lax.rsqrt(pa))
        out[c0 : c0 + 8, :] = jnp.where(lane <= c0 + sub, scaled, 0.0)


def split(x):
    a = x.astype(bf16)
    rest = x - a.astype(f32)
    b = rest.astype(bf16)
    return a, b, (rest - b.astype(f32)).astype(bf16)


def product(x, y, transposed=True):
    c = 1 if transposed else 0
    one = lambda a, b: lax.dot_general(a, b, (((1,), (c,)), ((), ())), preferred_element_type=f32)
    two = jnp.concatenate([y[0], y[1]], axis=1 - c)
    n = two.shape[1 - c] // 2
    high, mid = one(x[0], two), one(x[1], two)
    return ((one(x[0], y[2]) + one(x[2], y[0])) + mid[:, n:]) + (mid[:, :n] + high[:, n:]) + high[:, :n]


def at(i):
    return slice(i * B, i * B + B)


def means_of(expo):
    lane = lax.broadcasted_iota(jnp.int32, (B, B), 1)
    upto = jnp.where(lax.broadcasted_iota(jnp.int32, (B, B), 0) <= lane, 1.0, 0.0).astype(f32)
    sums = dot(expo, upto, 1, 0)
    before = jnp.zeros((1, 1), f32)
    parts = []
    for i in range(K // B):
        parts.append(sums[i : i + 1, :] + before)
        before = before + sums[i : i + 1, B - 1 : B]
    place = lax.broadcasted_iota(jnp.int32, (K // B, B), 0) * B + lax.broadcasted_iota(jnp.int32, (K // B, B), 1)
    return jnp.concatenate(parts, axis=0) / (place + 1).astype(f32)


def sweep_kernel(
    cuts, levels, basis, handed, exponents, running,
    lev, start, ins, prop, gat, part, other, near, far, across, slab, x, piv, allp, ls, xs, cs, lis, inv, ones,
    gs, gr, fs, g2r, ps, pr, ns, nr, nis, nir, f3s, f3r, f3is, f3ir, f4s, f4r, f4is, f4ir,
    als, alr, xss, xrs, vs, vr,
):
    me = lax.axis_index("col")
    c = lax.axis_index("cuts")
    z, h = me // 2, me % 2
    up, down = lax.rem(z + 1, CHIPS), lax.rem(z + CHIPS - 1, CHIPS)
    partner = z * 2 + 1 - h
    mine = pl.ds(pl.multiple_of(h * HALF, HALF), HALF)
    theirs = pl.ds(pl.multiple_of((1 - h) * HALF, HALF), HALF)
    my_cols = pl.ds(pl.multiple_of(me * B, B), B)
    my_rows = pl.ds(pl.multiple_of(me * HALF, HALF), HALF)
    blocks = K // B
    sends = []
    loads = [pltpu.make_async_copy(levels, lev, ins.at[0]), pltpu.make_async_copy(basis, start, ins.at[1])]
    for load in loads:
        load.start()

    barrier = pltpu.get_barrier_semaphore()
    for o in range(1, COL):
        pl.semaphore_signal(barrier, inc=1, device_id={"col": lax.rem(me + o, COL)}, device_id_type=MESH)
    inner = min(8, cuts)
    outer = cuts // inner
    cx, cy = c // inner, c % inner
    stages = (
        (inner, 0, cy, lambda o: cx * inner + lax.rem(cy + o, inner)),
        (outer, inner, cx, lambda o: lax.rem(cx + o, outer) * inner + cy),
    )
    for count, _, _, mate in stages:
        for o in range(1, count):
            pl.semaphore_signal(barrier, inc=1, device_id={"cuts": mate(o), "col": me}, device_id_type=MESH)

    @pl.when(c > 0)
    def _():
        for i in range(COL):
            pl.semaphore_signal(barrier, inc=1, device_id={"cuts": c - 1, "col": i}, device_id_type=MESH)

    for load in loads:
        load.wait()
    upper = start[:, :SITES]
    lower = start[:, SITES:]
    for n in range(SLICES):
        onsite = disorder * (lev[n : n + 1, :].astype(f32) / level_span - 0.5)
        upper, lower = (energy - onsite) * upper - neighbours(upper) - lower, upper
    prop[:, :SITES] = upper
    prop[:, SITES:] = lower

    @pl.when(c == 0)
    def _():
        handed[...] = start[...]

    everyone = COL - 1 + inner - 1 + outer - 1
    pl.semaphore_wait(barrier, jnp.where(c < cuts - 1, everyone + COL, everyone))

    their_half = pl.ds(pl.multiple_of((1 - h) * SITES, SITES), SITES)
    swap = remote(prop.at[:, their_half], gat.at[0, mine], gs.at[4], gr.at[h], {"col": partner})
    swap.start()
    sends.append(swap)
    for way in range(2):
        for t, (slot, chip) in enumerate(((1, up), (3, down))):
            f = h if way == 0 else 1 - h
            half = prop.at[:, pl.ds(pl.multiple_of(f * SITES, SITES), SITES)]
            out = remote(half, gat.at[slot, mine], gs.at[2 * way + t], gr.at[2 * slot + h], {"col": chip * 2 + f})
            out.start()
            sends.append(out)
    gat[0, mine, :] = prop[:, pl.ds(pl.multiple_of(h * SITES, SITES), SITES)]

    def come(ref, sem):
        remote(ref, ref, gs.at[0], sem, {"col": partner}).wait_recv()

    def arrived(slot, s):
        come(gat.at[slot, pl.ds(pl.multiple_of(s * HALF, HALF), HALF)], gr.at[2 * slot + s])

    kinds = ((0, 0, 0, 0), (0, 1, 0, 3), (-1, 2, 1, 3), (-1, 3, 1, 4), (-2, 3, 2, 3), (-2, 4, 2, 4))

    def make(kind):
        offset, d, one, two = kinds[kind]
        if d == 0:
            value = dot(gat[one], gat[one], 1, 1)
        else:
            wraps = lax.rem(z + CHIPS + offset, CHIPS) + d >= CHIPS
            value = dot(gat[jnp.where(wraps, one, two)], gat[jnp.where(wraps, two, one)], 1, 1)
        part[:, kind * B : kind * B + B] = value

    def pair_sum(group, lo, hi):
        cols = pl.ds(lo * B, (hi - lo) * B)
        both = remote(part.at[theirs, cols], other.at[:, cols], ps.at[group], pr.at[group], {"col": partner})
        both.start()
        both.wait_recv()
        sends.append(both)
        return part[mine, lo * B : hi * B] + other[:, lo * B : hi * B]

    quarter = HALF // 2
    halves = [pl.ds(pl.multiple_of(h * HALF + q * quarter, quarter), quarter) for q in range(2)]
    their_halves = [pl.ds(pl.multiple_of((1 - h) * HALF + q * quarter, quarter), quarter) for q in range(2)]

    def near_step(d):
        rows = (mine, mine) if d < 4 else halves
        for way, (chip, to) in enumerate(
            ((lax.rem(z + CHIPS - d + 1, CHIPS), up), (lax.rem(z + d - 1, CHIPS), down))
        ):
            ref = near.at[chip, rows[way]]
            out = remote(ref, ref, ns.at[2 * d + way], nr.at[2 * d + way], {"col": to * 2 + h})
            out.start()
            sends.append(out)

    def near_inside(chip, rows, i):
        ref = near.at[chip, rows]
        out = remote(ref, ref, nis.at[i], nir.at[i], {"col": partner})
        out.start()
        sends.append(out)

    def near_chips(d):
        return lax.rem(z + CHIPS - d, CHIPS), lax.rem(z + d, CHIPS)

    def near_come(d):
        rows = (mine, mine) if d < 4 else halves
        for way, chip in enumerate(near_chips(d)):
            come(near.at[chip, rows[way]], nr.at[2 * d + way])
            near_inside(chip, rows[way], 2 * d + way)

    def far_place(way):
        return lax.rem(z + CHIPS - way, CHIPS)

    def far_out(way, o):
        ref = far.at[far_place(way), mine]
        to = lax.rem(z + (o if way else CHIPS - o), CHIPS)
        return remote(ref, ref, f3s.at[4 * way + o], f3r.at[4 * way + o], {"col": to * 2 + h})

    def far_from(way, o):
        return lax.rem(z + (CHIPS - o - 1 if way else o), CHIPS)

    def far_inside(way, o):
        ref = far.at[far_from(way, o), mine]
        return remote(ref, ref, f3is.at[4 * way + o], f3ir.at[4 * way + o], {"col": partner})

    steps4 = (1, CHIPS - 1, 2 + 4 * h)

    def across_of(chip):
        return lax.rem(chip + CHIPS - 2, CHIPS // 2)

    def across_out(i):
        ref = across.at[across_of(z), mine]
        return remote(ref, ref, f4s.at[i], f4r.at[i], {"col": lax.rem(z + steps4[i], CHIPS) * 2 + h})

    def across_from(i):
        return across_of(z) if i == 3 else across_of(lax.rem(z + CHIPS - steps4[i], CHIPS))

    def across_inside(i):
        ref = across.at[across_from(i), mine]
        return remote(ref, ref, f4is.at[i], f4ir.at[i], {"col": partner})

    def piece(n):
        s = h if n < 2 else 1 - h
        return pl.ds(pl.multiple_of(s * HALF + n % 2 * quarter, quarter), quarter)

    def second_hop(n):
        for way, (slot, chip) in enumerate(((1, up), (3, down))):
            out = remote(
                gat.at[slot, piece(n)], gat.at[slot + 1, piece(n)], fs.at[4 * way + n], g2r.at[4 * way + n],
                {"col": chip * 2 + h},
            )
            out.start()
            sends.append(out)

    def far_issue():
        for n in range(4):
            for way in range(2):
                come(gat.at[2 * way + 2, piece(n)], g2r.at[4 * way + n])
        make(3)
        make(4)
        make(5)
        late = pair_sum(2, 3, 6)
        far[far_place(0), mine, :] = late[:, :B]
        far[far_place(1), mine, :] = late[:, B : 2 * B]
        across[across_of(z), mine, :] = late[:, 2 * B :]
        for o in range(1, 4):
            far_out(0, o).start()
            far_out(1, o).start()
            if o < 3:
                across_out(o - 1).start()
        across_out(2).start()
        far_inside(0, 0).start()
        far_inside(1, 0).start()
        across_inside(3).start()

    def far_finish():
        for o in range(1, 4):
            for way in range(2):
                come(far.at[far_from(way, o), mine], f3r.at[4 * way + o])
                far_inside(way, o).start()
        for i in range(3):
            come(across.at[across_from(i), mine], f4r.at[i])
            across_inside(i).start()

    def far_complete():
        for o in range(4):
            for way in range(2):
                come(far.at[far_from(way, o), theirs], f3ir.at[4 * way + o])
        for i in range(4):
            n = across_of(z) if i == 3 else across_of(lax.rem(z + CHIPS - (1, CHIPS - 1, 6 - 4 * h)[i], CHIPS))
            come(across.at[n, theirs], f4ir.at[i])

    def columns_issue():
        for o in range(1, COL):
            out = columns_out(o)
            out.start()
            sends.append(out)
        slab[my_rows, :] = prop[:, my_cols]

    def gram_block(i, j):
        d = i - j
        if d <= 2 or d >= 6:
            chip, kind = (j, j, j + 1, 0, 0, 0, i + 1, i)[d], min(d, CHIPS - d)
            return near[chip % CHIPS, :, at(kind)]
        if d == 4:
            return across[j]
        return far[((j if d == 3 else i) + 1) % CHIPS]

    def columns_out(o):
        d = lax.rem(me + o, COL)
        cols = pl.ds(pl.multiple_of(d * B, B), B)
        return remote(prop.at[:, cols], slab.at[my_rows], als.at[o], alr.at[o], {"col": d})

    def rows_out(i):
        return remote(
            x.at[pl.ds(i * HALF, HALF)], handed.at[:, my_cols], xss.at[i], xrs.at[me], {"cuts": c + 1, "col": i}
        )

    come(gat.at[0, theirs], gr.at[1 - h])
    make(0)

    near[z, mine, 0:B] = pair_sum(0, 0, 1)

    arrived(1, h)
    arrived(3, h)
    second_hop(0)
    arrived(1, 1 - h)
    arrived(3, 1 - h)
    make(1)
    make(2)
    near[z, mine, B : 3 * B] = pair_sum(1, 1, 3)
    near_step(1)
    second_hop(1)
    near_inside(z, mine, 0)
    near_come(1)
    near_step(2)
    second_hop(2)

    near_come(2)
    near_step(3)
    second_hop(3)
    near_come(3)
    near_step(4)
    far_issue()
    columns_issue()
    near_come(4)
    for d in range(5):
        rows = (theirs, theirs) if d < 4 else their_halves
        for way, chip in enumerate(near_chips(d)):
            if d or way == 0:
                come(near.at[chip, rows[way]], nir.at[2 * d + way])

    ones[...] = jnp.ones_like(ones)
    one = ones[...]

    eye = lax.broadcasted_iota(jnp.int32, (B, B), 0) == lax.broadcasted_iota(jnp.int32, (B, B), 1)
    three = range(3)

    def known(k):
        done = slice(0, k * B)
        xp = slab[at(k), :]
        if k:
            xp = xp - product([ls[s, at(k), done] for s in three], [xs[s, done, :] for s in three], False)
        return xp

    def solve(k, xp, inverse):
        solved = product(inverse, split(xp), False)
        x[at(k), :] = solved * math.sqrt(ROWS)
        if k < blocks - 1:
            solved = split(solved)
            for s in three:
                xs[s, at(k), :] = solved[s]

    def hand_over(ks):
        @pl.when(c < cuts - 1)
        def _():
            for k in ks:
                rows_out(2 * k).start()
                rows_out(2 * k + 1).start()

    for k in range(blocks):
        done = slice(0, k * B)
        top = WAIT + 1 if k < WAIT else blocks
        rest = slice((k + 1) * B, top * B)
        if k == WAIT:
            far_finish()
            far_complete()
        if k == LAG:
            for o in range(1, COL):
                rows = pl.ds(pl.multiple_of(lax.rem(me + COL - o, COL) * HALF, HALF), HALF)
                come(slab.at[rows], alr.at[o])
        if k:
            before = (WAIT + 1 if k <= WAIT else blocks) * B
            column = split(product(split(cs[k * B : before, :]), li))
            for s in three:
                ls[s, k * B : before, at(k - 1)] = column[s]
        if k == WAIT:
            low = slice((WAIT + 1) * B, K)
            for j in range(WAIT):
                early = slice(0, j * B)
                column = jnp.concatenate([gram_block(i, j) for i in range(WAIT + 1, blocks)], axis=0)
                if j:
                    column = column - product([ls[s, low, early] for s in three], [ls[s, at(j), early] for s in three])
                column = split(product(split(column), [lis[s, j] for s in three]))
                for s in three:
                    ls[s, low, at(j)] = column[s]
        if k:
            lk = [ls[s, at(k), done] for s in three]
        if k == LAG:
            for j in range(k):
                solve(j, known(j), [lis[s, j] for s in three])
        if k >= LAG:
            xp = known(k)
        if k < blocks - 1:
            later = gram_block(k + 1, k + 1)
            if k:
                taken = product([ls[s, rest, done] for s in three], lk)
                for i in range(k + 1, top):
                    cs[at(i), :] = gram_block(i, k) - taken[at(i - k - 1), :]
            else:
                for i in range(1, top):
                    cs[at(i), :] = gram_block(i, 0)
            if k:
                ln = [ls[s, at(k + 1), done] for s in three]
                later = later - product(ln, ln)
        if k == 0:
            d = gram_block(0, 0)
        eliminate(d, inv, one)
        inverse = inv[...]
        li = split(inverse)
        if k < blocks - 1:
            l1 = split(product(split(cs[at(k + 1), :]), li))
            d = later - product(l1, l1)
        if k >= LAG:
            solve(k, xp, li)
        else:
            for s in three:
                lis[s, k] = li[s]
        diagonal = jnp.sum(jnp.where(eye, inverse, 0.0), axis=0, keepdims=True)
        piv[k : k + 1, :] = -jnp.log(diagonal) - 0.5 * math.log(ROWS)
        if k >= LAG:
            hand_over(range(k + 1) if k == LAG else (k,))

    give = []
    total = piv[...]
    for count, base, position, mate in stages:
        allp[base + position] = total
        ref = allp.at[base + position]
        for o in range(1, count):
            out = remote(ref, ref, vs.at[base + o], vr.at[base + o], {"cuts": mate(o), "col": me})
            out.start()
            give.append(out)
        for o in range(1, count):
            come(allp.at[base + lax.rem(position + count - o, count)], vr.at[base + o])
        total = tree([allp[base + i] for i in range(count)])
    expo = total / (SLICES * cuts)
    means = means_of(expo)
    here = lax.broadcasted_iota(jnp.int32, (K // B, B), 0) == z
    for value, out in ((expo, exponents), (means, running)):
        line = jnp.sum(jnp.where(here, value, 0.0), axis=0, keepdims=True)
        out[...] = jnp.where(h == 0, line[:, :HALF], line[:, HALF:])

    @pl.when(c > 0)
    def _():
        for j in range(COL):
            come(handed.at[:, pl.ds(j * B, B)], xrs.at[j])

    @pl.when(c < cuts - 1)
    def _():
        for i in range(COL):
            rows_out(i).wait_send()

    for way in range(2):
        for o in range(4):
            if o:
                far_out(way, o).wait_send()
            far_inside(way, o).wait_send()
    for i in range(4):
        if i < 3:
            across_out(i).wait_send()
        across_inside(i).wait_send()
    for s in sends + give:
        s.wait_send()


def local(cuts, levels, start_basis):
    start = start_basis[0]
    dma = pltpu.SemaphoreType.DMA
    handed, exponents, running = pl.pallas_call(
        functools.partial(sweep_kernel, cuts),
        out_shape=(
            jax.ShapeDtypeStruct((HALF, ROWS), f32),
            jax.ShapeDtypeStruct((1, HALF), f32),
            jax.ShapeDtypeStruct((1, HALF), f32),
        ),
        in_specs=[pl.BlockSpec(memory_space=pl.ANY)] * 2,
        out_specs=(VMEM,) * 3,
        scratch_shapes=[
            pltpu.VMEM((SLICES, SITES), jnp.int32),
            pltpu.VMEM((HALF, ROWS), f32),
            dma((2,)),
            pltpu.VMEM((HALF, ROWS), f32),
            pltpu.VMEM((5, B, SITES), f32),
            pltpu.VMEM((B, BANDS), f32),
            pltpu.VMEM((HALF, BANDS), f32),
            pltpu.VMEM((CHIPS, B, 3 * B), f32),
            pltpu.VMEM((CHIPS, B, B), f32),
            pltpu.VMEM((CHIPS // 2, B, B), f32),
            pltpu.VMEM((K, B), f32),
            pltpu.VMEM((K, B), f32),
            pltpu.VMEM((K // B, B), f32),
            pltpu.VMEM((cuts + 1, K // B, B), f32),
            pltpu.VMEM((3, K, K), bf16),
            pltpu.VMEM((3, K, B), bf16),
            pltpu.VMEM((K, B), f32),
            pltpu.VMEM((3, max(LAG, 1), B, B), bf16),
            pltpu.VMEM((B, B), f32),
            pltpu.VMEM((8, B), f32),
            dma((5,)), dma((10,)), dma((8,)), dma((8,)), dma((3,)), dma((3,)),
            dma((10,)), dma((10,)), dma((10,)), dma((10,)),
            dma((CHIPS,)), dma((CHIPS,)), dma((CHIPS,)), dma((CHIPS,)), dma((3,)), dma((3,)), dma((4,)), dma((4,)),
            dma((COL,)), dma((COL,)), dma((COL,)), dma((COL,)), dma((cuts + 1,)), dma((cuts + 1,)),
        ],
        compiler_params=pltpu.CompilerParams(
            collective_id=1, has_side_effects=True, vmem_limit_bytes=48 << 20
        ),
        name="sweep",
    )(levels, start)
    return exponents[0], running[0], handed[None]


def solution(mesh):
    in_specs = (P("cuts", None), P("cuts", "col", None))
    out_specs = (P("col"), P("col"), P("cuts", "col", None))
    return jax.shard_map(
        functools.partial(local, mesh.shape["cuts"]), mesh=mesh, in_specs=in_specs, out_specs=out_specs, check_vma=False
    )
```
